128 devices in a mesh: dp: 16 (over y, x_hi, core), tensor: 8 (over z, x_lo).
Axes of the slice: x: 4 (x_hi: 2, x_lo: 2; x = x_hi * 2 + x_lo), y: 4, z: 4, core: 2. Of those that a mesh axis runs over, the one named last changes fastest.
Arguments:
- hidden_acts: bfloat16 [16384, 14336], P('dp', 'tensor'), may hold values from -6 to 6
- act_basis: bfloat16 [14336, 1024], P('tensor'), may hold values from -0.046875 to 0.046875
- out_grads: bfloat16 [16384, 4096], P('dp', 'tensor'), may hold values from -6 to 6
- grad_basis: bfloat16 [4096, 1024], P('tensor'), may hold values from -0.09375 to 0.09375
- routed: int32 [16384], P('dp'), may hold values 0 or 1
Outputs:
- act_gram: float32 [1024, 1024], P('dp', 'tensor')
- grad_gram: float32 [1024, 1024], P('dp', 'tensor')
- correction: float32 [1024, 1024], P('dp', 'tensor')
The draws below stay inside these ranges and needn't reach their ends.
All inputs are finite; a program needn't handle non-finite values. No bound on the sum of `routed` on one device may be relied on, other than what follows from the above.
Results may differ from the reference program's by a relative error of at most 0.0014.
Values may be sent and summed in bfloat16 or wider, within the bound.
No kernel may reach another device: no remote copies, remote signals or barrier semaphores. Data moves between devices by JAX's collectives and lax.ppermute only.
A program may use at most 64 MiB of HBM per device.

```python
import jax
import jax.numpy as jnp

D = 4096
FF = 14336
R = 1024
TOKENS = 16384


def plant(values, own_key, least, largest):
    longest = values.shape.index(max(values.shape))
    spots = []
    for shift in (0, 1):
        where = [jax.random.randint(jax.random.fold_in(own_key, axis), (), 0, length) for axis, length in enumerate(values.shape)]
        where[longest] = (where[longest] + shift) % values.shape[longest]
        spots.append(tuple(where))
    return values.at[spots[0]].set(least).at[spots[1]].set(largest)


def block_levels(key, extent, pieces, least, top_value):
    def one(axis_at, blocks):
        draws = jax.random.uniform(jax.random.fold_in(jax.random.fold_in(key, 6), axis_at), (blocks,), jnp.float32, least / len(pieces), top_value / len(pieces))
        return jnp.repeat(jnp.exp(draws), extent[axis_at] // blocks).reshape((-1,) + (1,) * (len(extent) - axis_at - 1))

    gain = one(*pieces[0])
    for cut in pieces[1:]:
        gain = gain * one(*cut)
    return gain


def bell_draw(stream_key, extent, deviation, reach, pieces=(), dtype=jnp.bfloat16):
    array = jax.random.normal(stream_key, extent, jnp.float32) * deviation
    if len(pieces) > 0:
        array = block_levels(stream_key, extent, pieces, -0.22, 0.18) * array
    return jnp.clip(array, min=-reach, max=reach).astype(dtype)


def setup_inputs(seed: int = 0) -> dict:
    streams_of = jax.random.split(jax.random.key(seed), 6)
    return {
        "hidden_acts": bell_draw(streams_of[0], (TOKENS, FF), 1.0, 6.0, ((0, 16), (1, 8))),
        "act_basis": bell_draw(streams_of[1], (FF, R), FF ** -0.5, 0.046875, ((0, 8),)),
        "out_grads": bell_draw(streams_of[2], (TOKENS, D), 1.0, 6.0, ((0, 16), (1, 8))),
        "grad_basis": bell_draw(streams_of[3], (D, R), D ** -0.5, 0.09375, ((0, 8),)),
        "routed": plant((jax.random.randint(streams_of[4], (TOKENS,), 0, 2) < 1).astype(jnp.int32), jax.random.fold_in(streams_of[4], 1), 0, 1),
    }


def rotate(values, basis):
    return jnp.dot(values, basis, preferred_element_type=jnp.float32).astype(jnp.bfloat16)


def reference(hidden_acts, act_basis, out_grads, grad_basis, routed):
    rot_acts = rotate(hidden_acts, act_basis)
    rot_grads = rotate(out_grads, grad_basis)
    weights = routed.astype(jnp.float32)[:, None]
    acts_f = rot_acts.astype(jnp.float32)
    grads_f = rot_grads.astype(jnp.float32)
    masked_acts = (acts_f * weights).astype(jnp.bfloat16)
    masked_grads = (grads_f * weights).astype(jnp.bfloat16)
    sq_acts = (acts_f * acts_f * weights).astype(jnp.bfloat16)
    sq_grads = (grads_f * grads_f).astype(jnp.bfloat16)
    scale = 1.0 / TOKENS
    act_gram = jnp.dot(masked_acts.T, rot_acts, preferred_element_type=jnp.float32) * scale
    grad_gram = jnp.dot(masked_grads.T, rot_grads, preferred_element_type=jnp.float32) * scale
    correction = jnp.dot(sq_acts.T, sq_grads, preferred_element_type=jnp.float32) * scale
    return act_gram, grad_gram, correction
```

```python
import jax
import jax.numpy as jnp
from jax import lax
from jax.experimental import pallas as pl
from jax.experimental.pallas import tpu as pltpu
from jax.sharding import Mesh
from jax.sharding import PartitionSpec as P

BF = jnp.bfloat16
F32 = jnp.float32
I16 = jnp.int16

SLOT = 72
KEEP = SLOT - 1
BLOCKS = 8
ROWS = SLOT * BLOCKS
CAP = KEEP * BLOCKS
TOP = 32767.0
HOPS = (1, 3, 2)
VMEM = pltpu.CompilerParams(vmem_limit_bytes=56 * 1024 * 1024)


def ring(dist):
    return [(i, (i + dist) % 4) for i in range(4)]


SWAP = [(0, 1), (1, 0)]


def last_row(shape):
    return lax.broadcasted_iota(jnp.int32, shape, len(shape) - 2) % SLOT == KEEP


def exponent_of(top):
    return jnp.clip(jnp.ceil(jnp.log2(jnp.maximum(top, 1e-37))), -100.0, 100.0)


def encode(x, k):
    y = x * jnp.exp2(-k)
    mag = jnp.abs(y)
    root = y * lax.rsqrt(jnp.maximum(mag, 1e-30))
    q = jnp.round(jnp.clip(root * TOP, -TOP, TOP))
    q = jnp.where(last_row(x.shape), k, q)
    return q.astype(jnp.int32).astype(I16)


def decode(q):
    q = q.astype(F32)
    unit = jnp.exp2(q[KEEP:SLOT, :]) * (1.0 / (TOP * TOP))
    x = q * jnp.abs(q) * unit
    return jnp.where(last_row(x.shape), 0.0, x)


def top_of(x):
    return jnp.max(jnp.max(jnp.abs(x), axis=1, keepdims=True), axis=0, keepdims=True)


def ranks(routed):
    r = routed.astype(F32).astype(BF)
    i = lax.broadcasted_iota(jnp.int32, (128, 128), 0)
    j = lax.broadcasted_iota(jnp.int32, (128, 128), 1)
    within = jnp.dot(r, (i <= j).astype(F32).astype(BF), preferred_element_type=F32)
    totals = jnp.dot(r, jnp.ones((128, 128), BF), preferred_element_type=F32)
    before = jnp.zeros((1, 128), F32)
    offs = []
    for row in range(8):
        offs.append(before)
        before = before + totals[row : row + 1, :]
    pos = within + jnp.concatenate(offs, axis=0) - 1.0
    return jnp.where(routed > 0, pos, -1.0), before


def build_select(sel_ref, pos, blocks):
    row = lax.broadcasted_iota(jnp.int32, (ROWS, 128), 0)
    base = jnp.zeros((ROWS, 128), jnp.int32)
    for b, q in enumerate(blocks):
        inside = (row >= b * SLOT) & (row < (b + 1) * SLOT)
        base = jnp.where(inside, q * KEEP - b * SLOT, base)
    want = jnp.where(row % SLOT == KEEP, -2, base + row).astype(F32)
    for c in range(8):
        sel_ref[:, c * 128 : (c + 1) * 128] = (want == pos[c : c + 1, :]).astype(F32).astype(BF)


def grads_kernel(routed_ref, g_ref, b_ref, send_ref, keep_ref, sel_ref, out_ref):
    z, xl = lax.axis_index("z"), lax.axis_index("xl")
    pos, _ = ranks(routed_ref[...])
    zs = [lax.rem(z + d, 4) for d in (0,) + HOPS]
    build_select(sel_ref, pos, [zz * 2 + (1 - xl) for zz in zs] + [zz * 2 + xl for zz in zs])
    picked = jnp.dot(sel_ref[...], g_ref[...], preferred_element_type=F32).astype(BF)
    out_ref[...] = jnp.dot(picked, b_ref[...], preferred_element_type=F32)
    k = exponent_of(top_of(out_ref[: 4 * SLOT, :]))
    for b in range(4):
        send_ref[b] = encode(out_ref[b * SLOT : (b + 1) * SLOT, :], k)
        keep_ref[b] = out_ref[(4 + b) * SLOT : (5 + b) * SLOT, :]


def acts_kernel(routed_ref, h_ref, b_ref, s1_ref, s2_ref, s3_ref, keep_ref, bad_ref, sel_ref, out_ref):
    step = pl.program_id(0)

    @pl.when(step == 0)
    def _():
        z, xl = lax.axis_index("z"), lax.axis_index("xl")
        pos, total = ranks(routed_ref[...])
        bad_ref[...] = jnp.broadcast_to(jnp.where(total > CAP, jnp.nan, 0.0), (8, 128))
        blocks = []
        for d in HOPS + (0,):
            zz = lax.rem(z + d, 4)
            blocks += [zz * 2 + xl, zz * 2 + (1 - xl)]
        build_select(sel_ref, pos, blocks)

    picked = jnp.dot(sel_ref[...], h_ref[...], preferred_element_type=F32).astype(BF)
    part = jnp.dot(picked, b_ref[...], preferred_element_type=F32)

    @pl.when(step == 0)
    def _():
        out_ref[...] = part

    @pl.when(step > 0)
    def _():
        out_ref[...] += part

    @pl.when(step == pl.num_programs(0) - 1)
    def _():
        k = exponent_of(top_of(out_ref[: 6 * SLOT, :]))
        for b in range(2):
            for n, s_ref in enumerate((s1_ref, s2_ref, s3_ref)):
                at = (2 * n + b) * SLOT
                s_ref[b] = encode(out_ref[at : at + SLOT, :], k)
            keep_ref[b] = out_ref[(6 + b) * SLOT : (7 + b) * SLOT, :]


def grads_mid_kernel(keep_ref, got_ref, own_ref, s1_ref, s2_ref, s3_ref, tmp_ref):
    own_ref[...] = keep_ref[0] + decode(got_ref[0])
    for b in range(3):
        tmp_ref[b] = keep_ref[b + 1] + decode(got_ref[b + 1])
    top = top_of(tmp_ref[0])
    for b in (1, 2):
        top = jnp.maximum(top, top_of(tmp_ref[b]))
    k = exponent_of(top)
    for b, s_ref in enumerate((s1_ref, s2_ref, s3_ref)):
        s_ref[...] = encode(tmp_ref[b], k)


def acts_mid_kernel(keep_ref, r1_ref, r2_ref, r3_ref, own_ref, send_ref):
    own_ref[...] = keep_ref[0] + decode(r1_ref[0]) + decode(r2_ref[0]) + decode(r3_ref[0])
    other = keep_ref[1] + decode(r1_ref[1]) + decode(r2_ref[1]) + decode(r3_ref[1])
    send_ref[...] = encode(other, exponent_of(top_of(other)))


def grads_end_kernel(own_ref, r1_ref, r2_ref, r3_ref, rot_ref):
    x = own_ref[...] + decode(r1_ref[...]) + decode(r2_ref[...]) + decode(r3_ref[...])
    rot_ref[...] = x.astype(BF)


def acts_end_kernel(own_ref, got_ref, bad_ref, rot_ref):
    x = own_ref[...] + decode(got_ref[...]) + bad_ref[0:1, 0:1]
    rot_ref[...] = x.astype(BF)


PAD = 80


def gram_kernel(scale, a0, a1, a2, a3, g0, g1, g2, g3, out_ref, a_s, g_s):
    for s, refs in ((a_s, (a0, a1, a2, a3)), (g_s, (g0, g1, g2, g3))):
        for n, ref in enumerate(refs):
            s[n * PAD : n * PAD + SLOT, :] = ref[...]
            s[n * PAD + SLOT : (n + 1) * PAD, :] = jnp.zeros((PAD - SLOT, s.shape[1]), BF)
    y = lax.axis_index("y")
    rows = pl.ds(pl.multiple_of(y * 256, 256), 256)
    contract = (((0,), (0,)), ((), ()))

    def put(n, lhs, rhs):
        t = lax.dot_general(lhs, rhs, contract, preferred_element_type=F32) * scale
        t = t.astype(BF)
        for rb in range(4):
            for cb in range(8):
                out_ref[rb * 8 + cb, :, n * 128 : (n + 1) * 128] = t[rb * 64 : (rb + 1) * 64, cb * 128 : (cb + 1) * 128]

    def square(v):
        v = v.astype(F32)
        return (v * v).astype(BF)

    put(1, g_s[:, rows], g_s[...])
    put(0, a_s[:, rows], a_s[...])
    put(2, square(a_s[:, rows]), square(g_s[...]))


def final_kernel(in_ref, a_ref, g_ref, c_ref):
    t = in_ref[0].astype(F32)
    for n in range(1, 32):
        t = t + in_ref[n].astype(F32)
    a_ref[...] = t[:, :128]
    g_ref[...] = t[:, 128:256]
    c_ref[...] = t[:, 256:]


def sds(shape, dtype):
    return jax.ShapeDtypeStruct(shape, dtype)


def cost(flops, nbytes):
    return pl.CostEstimate(flops=flops, bytes_accessed=nbytes, transcendentals=0)


def fast(hidden_acts, act_basis, out_grads, grad_basis, routed):
    width = act_basis.shape[1]
    feats = hidden_acts.shape[1]
    tokens = hidden_acts.shape[0] * 16
    slots = routed.reshape(8, 128)
    blk = (SLOT, width)
    vmem = pl.BlockSpec(memory_space=pltpu.VMEM)

    g_send, g_keep = pl.pallas_call(
        grads_kernel,
        out_shape=(sds((4,) + blk, I16), sds((4,) + blk, F32)),
        in_specs=[vmem] * 3,
        out_specs=(vmem, vmem),
        scratch_shapes=[pltpu.VMEM((ROWS, 1024), BF), pltpu.VMEM((ROWS, width), F32)],
        compiler_params=VMEM,
        cost_estimate=cost(1_300_000_000, 4_000_000),
        name="grads",
    )(slots, out_grads, grad_basis)
    g_got = lax.ppermute(g_send, "xl", SWAP)

    step = 256
    *a_send, a_keep, bad = pl.pallas_call(
        acts_kernel,
        grid=(feats // step,),
        out_shape=(sds((2,) + blk, I16),) * 3 + (sds((2,) + blk, F32), sds((8, 128), F32)),
        in_specs=[
            pl.BlockSpec((8, 128), lambda i: (0, 0)),
            pl.BlockSpec((1024, step), lambda i: (0, i)),
            pl.BlockSpec((step, width), lambda i: (i, 0)),
        ],
        out_specs=(pl.BlockSpec((2,) + blk, lambda i: (0, 0, 0)),) * 4 + (pl.BlockSpec((8, 128), lambda i: (0, 0)),),
        scratch_shapes=[pltpu.VMEM((ROWS, 1024), BF), pltpu.VMEM((ROWS, width), F32)],
        compiler_params=VMEM,
        cost_estimate=cost(4_300_000_000, 9_000_000),
        name="acts",
    )(slots, hidden_acts, act_basis)
    a_got = [lax.ppermute(s, "z", ring(d)) for s, d in zip(a_send, HOPS)]

    g_own, *g_next = pl.pallas_call(
        grads_mid_kernel,
        out_shape=(sds(blk, F32),) + (sds(blk, I16),) * 3,
        in_specs=[vmem] * 2,
        out_specs=(vmem,) * 4,
        scratch_shapes=[pltpu.VMEM((3,) + blk, F32)],
        compiler_params=VMEM,
        name="grads_mid",
    )(g_keep, g_got)
    g_last = [lax.ppermute(s, "z", ring(d)) for s, d in zip(g_next, HOPS)]

    a_own, a_next = pl.pallas_call(
        acts_mid_kernel,
        out_shape=(sds(blk, F32), sds(blk, I16)),
        in_specs=[vmem] * 4,
        out_specs=(vmem,) * 2,
        compiler_params=VMEM,
        name="acts_mid",
    )(a_keep, *a_got)
    a_last = lax.ppermute(a_next, "xl", SWAP)

    rot_g = pl.pallas_call(
        grads_end_kernel,
        out_shape=sds(blk, BF),
        in_specs=[vmem] * 4,
        out_specs=vmem,
        compiler_params=VMEM,
        name="grads_end",
    )(g_own, *g_last)
    all_g = [rot_g] + [lax.ppermute(rot_g, "y", ring(d)) for d in HOPS]

    rot_a = pl.pallas_call(
        acts_end_kernel,
        out_shape=sds(blk, BF),
        in_specs=[vmem] * 3,
        out_specs=vmem,
        compiler_params=VMEM,
        name="acts_end",
    )(a_own, a_last, bad)
    all_a = [rot_a] + [lax.ppermute(rot_a, "y", ring(d)) for d in HOPS]

    parts = pl.pallas_call(
        lambda *refs: gram_kernel(1.0 / tokens, *refs),
        out_shape=sds((32, 64, 384), BF),
        in_specs=[vmem] * 8,
        out_specs=vmem,
        scratch_shapes=[pltpu.VMEM((4 * PAD, width), BF)] * 2,
        compiler_params=VMEM,
        name="gram",
    )(*all_a, *all_g)
    got = lax.all_to_all(parts, ("xh", "core", "z", "xl"), 0, 0, tiled=True)

    return pl.pallas_call(
        final_kernel,
        out_shape=(sds((64, 128), F32),) * 3,
        in_specs=[vmem],
        out_specs=(vmem,) * 3,
        compiler_params=VMEM,
        name="final",
    )(got)


DP = ("y", "xh", "core")
TENSOR = ("z", "xl")


def general(hidden_acts, act_basis, out_grads, grad_basis, routed):
    act_part = jnp.dot(hidden_acts, act_basis, preferred_element_type=F32)
    grad_part = jnp.dot(out_grads, grad_basis, preferred_element_type=F32)
    act_sum, grad_sum = lax.psum((act_part, grad_part), TENSOR)
    rot_acts = act_sum.astype(BF)
    rot_grads = grad_sum.astype(BF)
    total_tokens = rot_acts.shape[0] * 16
    weights = routed.astype(F32)[:, None]
    acts_f = rot_acts.astype(F32)
    grads_f = rot_grads.astype(F32)
    masked_acts = (acts_f * weights).astype(BF)
    masked_grads = (grads_f * weights).astype(BF)
    sq_acts = (acts_f * acts_f * weights).astype(BF)
    sq_grads = (grads_f * grads_f).astype(BF)
    col_width = rot_acts.shape[1] // 8
    col_start = (lax.axis_index("z") * 2 + lax.axis_index("xl")) * col_width
    own_rows = rot_acts.shape[1] // 16
    row_start = ((lax.axis_index("y") * 2 + lax.axis_index("xh")) * 2 + lax.axis_index("core")) * own_rows
    contract = (((0,), (0,)), ((), ()))
    terms = []
    for left, right in ((masked_acts, rot_acts), (masked_grads, rot_grads), (sq_acts, sq_grads)):
        cols = lax.dynamic_slice_in_dim(right, col_start, col_width, 1)
        terms.append(lax.dot_general(left, cols, contract, preferred_element_type=F32))
    summed = lax.psum(jnp.concatenate(terms, axis=1) * (1.0 / total_tokens), DP)
    owned = lax.dynamic_slice_in_dim(summed, row_start, own_rows, 0)
    return tuple(owned[:, n * col_width : (n + 1) * col_width] for n in range(3))


def shards(*args):
    act_gram, grad_gram, correction = fast(*args)
    whole = jnp.abs(act_gram[0, 0]) < 1e30
    return lax.cond(whole, lambda *_: (act_gram, grad_gram, correction), general, *args)


def solution(mesh):
    fine = Mesh(mesh.devices.reshape(4, 2, 2, 4, 2), ("y", "xh", "core", "z", "xl"))
    return jax.shard_map(
        shards,
        mesh=fine,
        in_specs=(P(DP, TENSOR), P(TENSOR, None), P(DP, TENSOR), P(TENSOR, None), P(DP)),
        out_specs=(P(DP, TENSOR),) * 3,
        check_vma=False,
    )
```

```python
import jax
import jax.numpy as jnp
from jax import lax
from jax.experimental import pallas as pl
from jax.experimental.pallas import tpu as pltpu
from jax.sharding import Mesh
from jax.sharding import PartitionSpec as P

BF = jnp.bfloat16
F32 = jnp.float32
I16 = jnp.int16

SLOT = 72
KEEP = SLOT - 1
BLOCKS = 8
CAP = KEEP * BLOCKS
TOP = 32767.0
HOPS = (1, 3, 2)


def ring(dist):
    return [(i, (i + dist) % 4) for i in range(4)]


SWAP = [(0, 1), (1, 0)]


def last_row(shape):
    return lax.broadcasted_iota(jnp.int32, shape, len(shape) - 2) % SLOT == KEEP


def exponent_of(top):
    return jnp.clip(jnp.ceil(jnp.log2(jnp.maximum(top, 1e-37))), -100.0, 100.0)


def encode(x, k):
    y = x * jnp.exp2(-k)
    mag = jnp.abs(y)
    root = y * lax.rsqrt(jnp.maximum(mag, 1e-30))
    q = jnp.round(jnp.clip(root * TOP, -TOP, TOP))
    q = jnp.where(last_row(x.shape), k, q)
    return q.astype(jnp.int32).astype(I16)


def decode(q):
    q = q.astype(F32)
    unit = jnp.exp2(q[KEEP:SLOT, :]) * (1.0 / (TOP * TOP))
    x = q * jnp.abs(q) * unit
    return jnp.where(last_row(x.shape), 0.0, x)


def top_of(x):
    return jnp.max(jnp.max(jnp.abs(x), axis=1, keepdims=True), axis=0, keepdims=True)


def ranks(routed):
    r = routed.astype(F32).astype(BF)
    i = lax.broadcasted_iota(jnp.int32, (128, 128), 0)
    j = lax.broadcasted_iota(jnp.int32, (128, 128), 1)
    within = jnp.dot(r, (i <= j).astype(F32).astype(BF), preferred_element_type=F32)
    totals = jnp.dot(r, jnp.ones((128, 128), BF), preferred_element_type=F32)
    before = jnp.zeros((1, 128), F32)
    offs = []
    for row in range(8):
        offs.append(before)
        before = before + totals[row : row + 1, :]
    pos = within + jnp.concatenate(offs, axis=0) - 1.0
    return jnp.where(routed > 0, pos, -1.0), before


def build_select(sel_ref, pos, blocks):
    rows = len(blocks) * SLOT
    row = lax.broadcasted_iota(jnp.int32, (rows, 128), 0)
    base = jnp.zeros((rows, 128), jnp.int32)
    for b, q in enumerate(blocks):
        inside = (row >= b * SLOT) & (row < (b + 1) * SLOT)
        base = jnp.where(inside, q * KEEP - b * SLOT, base)
    want = jnp.where(row % SLOT == KEEP, -2, base + row).astype(F32)
    for c in range(8):
        sel_ref[:, c * 128 : (c + 1) * 128] = (want == pos[c : c + 1, :]).astype(F32).astype(BF)


def grads_send_kernel(routed_ref, g_ref, b_ref, send_ref, sel_ref, out_ref):
    z, xl = lax.axis_index("z"), lax.axis_index("xl")
    pos, _ = ranks(routed_ref[...])
    build_select(sel_ref, pos, [lax.rem(z + d, 4) * 2 + (1 - xl) for d in (0,) + HOPS])
    picked = jnp.dot(sel_ref[...], g_ref[...], preferred_element_type=F32).astype(BF)
    out_ref[...] = jnp.dot(picked, b_ref[...], preferred_element_type=F32)
    k = exponent_of(top_of(out_ref[...]))
    for b in range(4):
        send_ref[b] = encode(out_ref[b * SLOT : (b + 1) * SLOT, :], k)


def grads_keep_kernel(routed_ref, g_ref, b_ref, after_ref, keep_ref, sel_ref):
    z, xl = lax.axis_index("z"), lax.axis_index("xl")
    pos, _ = ranks(routed_ref[...])
    build_select(sel_ref, pos, [lax.rem(z + d, 4) * 2 + xl for d in (0,) + HOPS])
    picked = jnp.dot(sel_ref[...], g_ref[...], preferred_element_type=F32).astype(BF)
    keep_ref[...] = jnp.dot(picked, b_ref[...], preferred_element_type=F32)


def acts_send_kernel(routed_ref, h_ref, b_ref, s1_ref, s2_ref, s3_ref, bad_ref, sel_ref, out_ref):
    z, xl = lax.axis_index("z"), lax.axis_index("xl")
    pos, total = ranks(routed_ref[...])
    bad_ref[...] = jnp.broadcast_to(jnp.where(total > CAP, jnp.nan, 0.0), (8, 128))
    blocks = []
    for d in HOPS:
        zz = lax.rem(z + d, 4)
        blocks += [zz * 2 + xl, zz * 2 + (1 - xl)]
    build_select(sel_ref, pos, blocks)
    picked = jnp.dot(sel_ref[...], h_ref[...], preferred_element_type=F32).astype(BF)
    out_ref[...] = jnp.dot(picked, b_ref[...], preferred_element_type=F32)
    k = exponent_of(top_of(out_ref[...]))
    for n, s_ref in enumerate((s1_ref, s2_ref, s3_ref)):
        for b in range(2):
            at = (2 * n + b) * SLOT
            s_ref[b] = encode(out_ref[at : at + SLOT, :], k)


def acts_keep_kernel(routed_ref, h_ref, b_ref, after_ref, keep_ref, sel_ref):
    z, xl = lax.axis_index("z"), lax.axis_index("xl")
    pos, _ = ranks(routed_ref[...])
    build_select(sel_ref, pos, [z * 2 + xl, z * 2 + (1 - xl)])
    picked = jnp.dot(sel_ref[...], h_ref[...], preferred_element_type=F32).astype(BF)
    keep_ref[...] = jnp.dot(picked, b_ref[...], preferred_element_type=F32)


def grads_mid_kernel(keep_ref, got_ref, own_ref, s1_ref, s2_ref, s3_ref, tmp_ref):
    own_ref[...] = keep_ref[:SLOT, :] + decode(got_ref[0])
    for b in range(3):
        tmp_ref[b] = keep_ref[(b + 1) * SLOT : (b + 2) * SLOT, :] + decode(got_ref[b + 1])
    top = top_of(tmp_ref[0])
    for b in (1, 2):
        top = jnp.maximum(top, top_of(tmp_ref[b]))
    k = exponent_of(top)
    for b, s_ref in enumerate((s1_ref, s2_ref, s3_ref)):
        s_ref[...] = encode(tmp_ref[b], k)


def acts_mid_kernel(keep_ref, r1_ref, r2_ref, r3_ref, after_ref, own_ref, send_ref):
    own_ref[...] = keep_ref[:SLOT, :] + decode(r1_ref[0]) + decode(r2_ref[0]) + decode(r3_ref[0])
    other = keep_ref[SLOT:, :] + decode(r1_ref[1]) + decode(r2_ref[1]) + decode(r3_ref[1])
    send_ref[...] = encode(other, exponent_of(top_of(other)))


def grads_end_kernel(own_ref, r1_ref, r2_ref, r3_ref, rot_ref):
    x = own_ref[...] + decode(r1_ref[...]) + decode(r2_ref[...]) + decode(r3_ref[...])
    rot_ref[...] = x.astype(BF)


def acts_end_kernel(own_ref, got_ref, bad_ref, rot_ref):
    x = own_ref[...] + decode(got_ref[...]) + bad_ref[0:1, 0:1]
    rot_ref[...] = x.astype(BF)


PAD = 80
GATHERED = 8
CONTRACT = (((0,), (0,)), ((), ()))


def gather_rows(dst_ref, refs):
    for n, ref in enumerate(refs):
        dst_ref[n * PAD : n * PAD + SLOT, :] = ref[...]
        dst_ref[n * PAD + SLOT : (n + 1) * PAD, :] = jnp.zeros((PAD - SLOT, dst_ref.shape[1]), BF)


def square(v):
    v = v.astype(F32)
    return (v * v).astype(BF)


def own_columns(x_ref):
    y, core = lax.axis_index("y"), lax.axis_index("core")
    i = lax.broadcasted_iota(jnp.int32, (256, 128), 0)
    j = lax.broadcasted_iota(jnp.int32, (256, 128), 1)
    pick = (i == j + jnp.where(j >= 64, 64, 0) + core * 64).astype(F32).astype(BF)
    x = x_ref[:, pl.ds(pl.multiple_of(y * 256, 256), 256)]
    return jnp.dot(x, pick, preferred_element_type=F32).astype(BF)


def put(out_ref, n, t):
    for xh in range(2):
        for cb in range(8):
            out_ref[xh * 8 + cb, :, n * 128 : (n + 1) * 128] = t[xh * 64 : (xh + 1) * 64, cb * 128 : (cb + 1) * 128]


def grads_gram_kernel(scale, *refs):
    *g_refs, out_ref, g_s = refs
    gather_rows(g_s, g_refs)
    t = lax.dot_general(own_columns(g_s), g_s[...], CONTRACT, preferred_element_type=F32) * scale
    put(out_ref, 0, t.astype(BF))


def acts_gram_kernel(scale, *refs):
    *in_refs, gram_ref, out_ref, a_s, g_s = refs
    gather_rows(a_s, in_refs[:GATHERED])
    gather_rows(g_s, in_refs[GATHERED:])
    own = own_columns(a_s)
    t = lax.dot_general(own, a_s[...], CONTRACT, preferred_element_type=F32) * scale
    put(out_ref, 0, t.astype(BF))
    t = lax.dot_general(square(own), square(g_s[...]), CONTRACT, preferred_element_type=F32) * scale
    put(out_ref, 2, t.astype(BF))
    out_ref[:, :, 128:256] = gram_ref[...]


def final_kernel(in_ref, a_ref, g_ref, c_ref):
    t = in_ref[0].astype(F32)
    for n in range(1, 16):
        t = t + in_ref[n].astype(F32)
    a_ref[...] = t[:, :128]
    g_ref[...] = t[:, 128:256]
    c_ref[...] = t[:, 256:]


def sds(shape, dtype):
    return jax.ShapeDtypeStruct(shape, dtype)


def call(kernel, name, out_shape, args, scratch=(), mib=16, flops=0, behind=0):
    vmem = pl.BlockSpec(memory_space=pltpu.VMEM)
    anywhere = pl.BlockSpec(memory_space=pl.ANY)
    outs = out_shape if isinstance(out_shape, tuple) else (out_shape,)
    size = sum(a.size * a.dtype.itemsize for a in args + tuple(outs))
    return pl.pallas_call(
        kernel,
        out_shape=out_shape,
        in_specs=[vmem] * (len(args) - behind) + [anywhere] * behind,
        out_specs=(vmem,) * len(out_shape) if isinstance(out_shape, tuple) else vmem,
        scratch_shapes=list(scratch),
        compiler_params=pltpu.CompilerParams(vmem_limit_bytes=mib * 1024 * 1024),
        cost_estimate=pl.CostEstimate(flops=flops, bytes_accessed=size, transcendentals=0),
        name=name,
    )(*args)


def fast(hidden_acts, act_basis, out_grads, grad_basis, routed):
    width = act_basis.shape[1]
    tokens = hidden_acts.shape[0] * 16
    slots = routed.reshape(8, 128)
    blk = (SLOT, width)
    scale = 1.0 / tokens

    def sel(n):
        return pltpu.VMEM((n * SLOT, 1024), BF)

    def wide(n):
        return pltpu.VMEM((n * SLOT, width), F32)

    g_send = call(
        grads_send_kernel, "grads_send", sds((4,) + blk, I16), (slots, out_grads, grad_basis), (sel(4), wide(4)), 16, 600_000_000
    )
    g_got = lax.ppermute(g_send, "xl", SWAP)

    *a_send, bad = call(
        acts_send_kernel,
        "acts_send",
        (sds((2,) + blk, I16),) * 3 + (sds((8, 128), F32),),
        (slots, hidden_acts, act_basis),
        (sel(6), wide(6)),
        24,
        3_200_000_000,
    )
    a_got = [lax.ppermute(s, "z", ring(d)) for s, d in zip(a_send, HOPS)]

    g_keep = call(
        grads_keep_kernel,
        "grads_keep",
        sds((4 * SLOT, width), F32),
        (slots, out_grads, grad_basis, bad),
        (sel(4),),
        16,
        600_000_000,
        behind=1,
    )
    a_keep = call(
        acts_keep_kernel,
        "acts_keep",
        sds((2 * SLOT, width), F32),
        (slots, hidden_acts, act_basis, bad),
        (sel(2),),
        24,
        1_100_000_000,
        behind=1,
    )

    g_own, *g_next = call(
        grads_mid_kernel,
        "grads_mid",
        (sds(blk, F32),) + (sds(blk, I16),) * 3,
        (g_keep, g_got),
        (pltpu.VMEM((3,) + blk, F32),),
    )
    g_last = [lax.ppermute(s, "z", ring(d)) for s, d in zip(g_next, HOPS)]

    a_own, a_next = call(
        acts_mid_kernel, "acts_mid", (sds(blk, F32), sds(blk, I16)), (a_keep, *a_got, g_own), behind=1
    )
    a_last = lax.ppermute(a_next, "xl", SWAP)

    def gathered(rot):
        near = [rot] + [lax.ppermute(rot, "y", ring(d)) for d in HOPS]
        return near + [lax.ppermute(r, "core", SWAP) for r in near]

    rot_g = call(grads_end_kernel, "grads_end", sds(blk, BF), (g_own, *g_last))
    all_g = gathered(rot_g)
    rot_a = call(acts_end_kernel, "acts_end", sds(blk, BF), (a_own, a_last, bad))
    all_a = gathered(rot_a)

    def rows():
        return pltpu.VMEM((GATHERED * PAD, width), BF)

    gram = call(
        lambda *refs: grads_gram_kernel(scale, *refs), "grads_gram", sds((16, 64, 128), BF), tuple(all_g), (rows(),), 16, 200_000_000
    )
    parts = call(
        lambda *refs: acts_gram_kernel(scale, *refs),
        "acts_gram",
        sds((16, 64, 384), BF),
        (*all_a, *all_g, gram),
        (rows(), rows()),
        16,
        400_000_000,
    )
    got = lax.all_to_all(parts, ("xh", "z", "xl"), 0, 0, tiled=True)
    return call(final_kernel, "final", (sds((64, 128), F32),) * 3, (got,))


DP = ("y", "xh", "core")
TENSOR = ("z", "xl")


def general(hidden_acts, act_basis, out_grads, grad_basis, routed):
    act_part = jnp.dot(hidden_acts, act_basis, preferred_element_type=F32)
    grad_part = jnp.dot(out_grads, grad_basis, preferred_element_type=F32)
    act_sum, grad_sum = lax.psum((act_part, grad_part), TENSOR)
    rot_acts = act_sum.astype(BF)
    rot_grads = grad_sum.astype(BF)
    total_tokens = rot_acts.shape[0] * 16
    weights = routed.astype(F32)[:, None]
    acts_f = rot_acts.astype(F32)
    grads_f = rot_grads.astype(F32)
    masked_acts = (acts_f * weights).astype(BF)
    masked_grads = (grads_f * weights).astype(BF)
    sq_acts = (acts_f * acts_f * weights).astype(BF)
    sq_grads = (grads_f * grads_f).astype(BF)
    col_width = rot_acts.shape[1] // 8
    col_start = (lax.axis_index("z") * 2 + lax.axis_index("xl")) * col_width
    own_rows = rot_acts.shape[1] // 16
    row_start = ((lax.axis_index("y") * 2 + lax.axis_index("xh")) * 2 + lax.axis_index("core")) * own_rows
    contract = (((0,), (0,)), ((), ()))
    terms = []
    for left, right in ((masked_acts, rot_acts), (masked_grads, rot_grads), (sq_acts, sq_grads)):
        cols = lax.dynamic_slice_in_dim(right, col_start, col_width, 1)
        terms.append(lax.dot_general(left, cols, contract, preferred_element_type=F32))
    summed = lax.psum(jnp.concatenate(terms, axis=1) * (1.0 / total_tokens), DP)
    owned = lax.dynamic_slice_in_dim(summed, row_start, own_rows, 0)
    return tuple(owned[:, n * col_width : (n + 1) * col_width] for n in range(3))


def shards(*args):
    act_gram, grad_gram, correction = fast(*args)
    whole = jnp.abs(act_gram[0, 0]) < 1e30
    return lax.cond(whole, lambda *_: (act_gram, grad_gram, correction), general, *args)


def solution(mesh):
    fine = Mesh(mesh.devices.reshape(4, 2, 2, 4, 2), ("y", "xh", "core", "z", "xl"))
    return jax.shard_map(
        shards,
        mesh=fine,
        in_specs=(P(DP, TENSOR), P(TENSOR, None), P(DP, TENSOR), P(TENSOR, None), P(DP)),
        out_specs=(P(DP, TENSOR),) * 3,
        check_vma=False,
    )
```

```python
import jax
import jax.numpy as jnp
from jax import lax
from jax.experimental import pallas as pl
from jax.experimental.pallas import tpu as pltpu
from jax.sharding import Mesh
from jax.sharding import PartitionSpec as P

BF = jnp.bfloat16
F32 = jnp.float32
I16 = jnp.int16

SLOT = 72
KEEP = SLOT - 1
BLOCKS = 8
CAP = KEEP * BLOCKS
TOP = 32767.0
HOPS = (1, 3, 2)


def ring(dist):
    return [(i, (i + dist) % 4) for i in range(4)]


SWAP = [(0, 1), (1, 0)]
WIDTH = 1024
AX = 256
AZ = WIDTH - AX


def last_row(shape):
    return lax.broadcasted_iota(jnp.int32, shape, len(shape) - 2) % SLOT == KEEP


def exponent_of(top):
    return jnp.clip(jnp.ceil(jnp.log2(jnp.maximum(top, 1e-37))), -100.0, 100.0)


def encode(x, k):
    y = x * jnp.exp2(-k)
    mag = jnp.abs(y)
    root = y * lax.rsqrt(jnp.maximum(mag, 1e-30))
    q = jnp.round(jnp.clip(root * TOP, -TOP, TOP))
    q = jnp.where(last_row(x.shape), k, q)
    return q.astype(jnp.int32).astype(I16)


def decode(q):
    q = q.astype(F32)
    unit = jnp.exp2(q[KEEP:SLOT, :]) * (1.0 / (TOP * TOP))
    x = q * jnp.abs(q) * unit
    return jnp.where(last_row(x.shape), 0.0, x)


def top_of(x):
    return jnp.max(jnp.max(jnp.abs(x), axis=1, keepdims=True), axis=0, keepdims=True)


def ranks(routed):
    r = routed.astype(F32).astype(BF)
    i = lax.broadcasted_iota(jnp.int32, (128, 128), 0)
    j = lax.broadcasted_iota(jnp.int32, (128, 128), 1)
    within = jnp.dot(r, (i <= j).astype(F32).astype(BF), preferred_element_type=F32)
    totals = jnp.dot(r, jnp.ones((128, 128), BF), preferred_element_type=F32)
    before = jnp.zeros((1, 128), F32)
    offs = []
    for row in range(8):
        offs.append(before)
        before = before + totals[row : row + 1, :]
    pos = within + jnp.concatenate(offs, axis=0) - 1.0
    return jnp.where(routed > 0, pos, -1.0), before


def build_select(sel_ref, pos, blocks):
    rows = len(blocks) * SLOT
    row = lax.broadcasted_iota(jnp.int32, (rows, 128), 0)
    base = jnp.zeros((rows, 128), jnp.int32)
    for b, q in enumerate(blocks):
        inside = (row >= b * SLOT) & (row < (b + 1) * SLOT)
        base = jnp.where(inside, q * KEEP - b * SLOT, base)
    want = jnp.where(row % SLOT == KEEP, -2, base + row).astype(F32)
    for c in range(8):
        sel_ref[:, c * 128 : (c + 1) * 128] = (want == pos[c : c + 1, :]).astype(F32).astype(BF)


def grads_send_kernel(routed_ref, g_ref, b_ref, send_ref, sel_ref, out_ref):
    z, xl = lax.axis_index("z"), lax.axis_index("xl")
    pos, _ = ranks(routed_ref[...])
    build_select(sel_ref, pos, [lax.rem(z + d, 4) * 2 + (1 - xl) for d in (0,) + HOPS])
    picked = jnp.dot(sel_ref[...], g_ref[...], preferred_element_type=F32).astype(BF)
    out_ref[...] = jnp.dot(picked, b_ref[...], preferred_element_type=F32)
    k = exponent_of(top_of(out_ref[...]))
    for b in range(4):
        send_ref[b] = encode(out_ref[b * SLOT : (b + 1) * SLOT, :], k)


def grads_keep_kernel(routed_ref, g_ref, b_ref, after_ref, keep_ref, sel_ref):
    z, xl = lax.axis_index("z"), lax.axis_index("xl")
    pos, _ = ranks(routed_ref[...])
    build_select(sel_ref, pos, [lax.rem(z + d, 4) * 2 + xl for d in (0,) + HOPS])
    picked = jnp.dot(sel_ref[...], g_ref[...], preferred_element_type=F32).astype(BF)
    keep_ref[...] = jnp.dot(picked, b_ref[...], preferred_element_type=F32)


def acts_send_kernel(routed_ref, h_ref, b_ref, s1_ref, s2_ref, s3_ref, x_ref, keep_ref, picked_ref, bad_ref, sel_ref, z_ref):
    z, xl = lax.axis_index("z"), lax.axis_index("xl")
    pos, total = ranks(routed_ref[...])
    bad_ref[...] = jnp.broadcast_to(jnp.where(total > CAP, jnp.nan, 0.0), (8, 128))
    zs = [lax.rem(z + d, 4) * 2 for d in (0,) + HOPS]
    build_select(sel_ref, pos, [zz + xl for zz in zs] + [zz + (1 - xl) for zz in zs])
    picked_ref[...] = jnp.dot(sel_ref[...], h_ref[...], preferred_element_type=F32).astype(BF)
    z_ref[...] = jnp.dot(picked_ref[...], b_ref[:, :AZ], preferred_element_type=F32)
    k = exponent_of(jnp.maximum(top_of(z_ref[SLOT : 4 * SLOT, :]), top_of(z_ref[5 * SLOT :, :])))
    for n, s_ref in enumerate((s1_ref, s2_ref, s3_ref)):
        for b in range(2):
            at = (1 + n + 4 * b) * SLOT
            s_ref[b] = encode(z_ref[at : at + SLOT, :], k)
    for b in range(2):
        keep_ref[b] = z_ref[4 * b * SLOT : (4 * b + 1) * SLOT, :]
    x = jnp.dot(picked_ref[4 * SLOT :, :], b_ref[:, AZ:], preferred_element_type=F32)
    k = exponent_of(top_of(x))
    for b in range(4):
        x_ref[b] = encode(x[b * SLOT : (b + 1) * SLOT, :], k)


def acts_keep_kernel(picked_ref, b_ref, keep_ref):
    keep_ref[...] = jnp.dot(picked_ref[: 4 * SLOT, :], b_ref[:, AZ:], preferred_element_type=F32)


def x_mid_kernel(g_keep, g_got, a_keep, a_got, own_ref, s1_ref, s2_ref, s3_ref, tmp_ref):
    def total(b):
        rows = slice(b * SLOT, (b + 1) * SLOT)
        return g_keep[rows, :] + decode(g_got[b]), a_keep[rows, :] + decode(a_got[b])

    g, a = total(0)
    own_ref[:, :WIDTH] = g
    own_ref[:, WIDTH:] = a
    top = jnp.zeros((1, 1), F32)
    for b in range(3):
        g, a = total(b + 1)
        tmp_ref[b, :, :WIDTH] = g
        tmp_ref[b, :, WIDTH:] = a
        top = jnp.maximum(top, jnp.maximum(top_of(g), top_of(a)))
    k = exponent_of(top)
    for b, s_ref in enumerate((s1_ref, s2_ref, s3_ref)):
        s_ref[...] = encode(tmp_ref[b], k)


def z_mid_kernel(keep_ref, r1_ref, r2_ref, r3_ref, after_ref, own_ref, send_ref):
    own_ref[...] = keep_ref[0] + decode(r1_ref[0]) + decode(r2_ref[0]) + decode(r3_ref[0])
    other = keep_ref[1] + decode(r1_ref[1]) + decode(r2_ref[1]) + decode(r3_ref[1])
    send_ref[...] = encode(other, exponent_of(top_of(other)))


def x_end_kernel(own_ref, r1_ref, r2_ref, r3_ref, bad_ref, rot_ref):
    x = own_ref[...] + decode(r1_ref[...]) + decode(r2_ref[...]) + decode(r3_ref[...])
    rot_ref[...] = (x + bad_ref[0:1, 0:1]).astype(BF)


def z_end_kernel(own_ref, got_ref, rot_ref):
    rot_ref[...] = (own_ref[...] + decode(got_ref[...])).astype(BF)


PAD = 80
GATHERED = 8
CONTRACT = (((0,), (0,)), ((), ()))


def gather_rows(dst_ref, cols, refs, part):
    for n, ref in enumerate(refs):
        dst_ref[n * PAD : n * PAD + SLOT, cols] = ref[:, part]
        dst_ref[n * PAD + SLOT : (n + 1) * PAD, cols] = jnp.zeros((PAD - SLOT, ref[:, part].shape[1]), BF)


def square(v):
    v = v.astype(F32)
    return (v * v).astype(BF)


def own_columns(x_ref):
    y, core = lax.axis_index("y"), lax.axis_index("core")
    i = lax.broadcasted_iota(jnp.int32, (256, 128), 0)
    j = lax.broadcasted_iota(jnp.int32, (256, 128), 1)
    pick = (i == j + jnp.where(j >= 64, 64, 0) + core * 64).astype(F32).astype(BF)
    x = x_ref[:, pl.ds(pl.multiple_of(y * 256, 256), 256)]
    return jnp.dot(x, pick, preferred_element_type=F32).astype(BF)


def put(out_ref, n, t):
    for xh in range(2):
        for cb in range(8):
            out_ref[xh * 8 + cb, :, n * 128 : (n + 1) * 128] = t[xh * 64 : (xh + 1) * 64, cb * 128 : (cb + 1) * 128]


def gram_kernel(scale, *refs):
    x_refs, z_refs = refs[:GATHERED], refs[GATHERED : 2 * GATHERED]
    out_ref, whole_ref, a_s, g_s = refs[2 * GATHERED :]
    marks = x_refs[0][0:8, 0:128].astype(F32)
    for ref in x_refs[1:]:
        marks = marks + ref[0:8, 0:128].astype(F32)
    whole_ref[...] = jnp.where(jnp.abs(marks) < 1e30, 1.0, 0.0)
    gather_rows(g_s, slice(0, WIDTH), x_refs, slice(0, WIDTH))
    gather_rows(a_s, slice(AZ, WIDTH), x_refs, slice(WIDTH, WIDTH + AX))
    gather_rows(a_s, slice(0, AZ), z_refs, slice(0, AZ))

    def dot(lhs, rhs):
        return (lax.dot_general(lhs, rhs, CONTRACT, preferred_element_type=F32) * scale).astype(BF)

    own = own_columns(a_s)
    put(out_ref, 1, dot(own_columns(g_s), g_s[...]))
    put(out_ref, 0, dot(own, a_s[...]))
    put(out_ref, 2, dot(square(own), square(g_s[...])))


def final_kernel(in_ref, a_ref, g_ref, c_ref):
    t = in_ref[0].astype(F32)
    for n in range(1, 16):
        t = t + in_ref[n].astype(F32)
    a_ref[...] = t[:, :128]
    g_ref[...] = t[:, 128:256]
    c_ref[...] = t[:, 256:]


def sds(shape, dtype):
    return jax.ShapeDtypeStruct(shape, dtype)


def call(kernel, name, out_shape, args, scratch=(), mib=16, flops=0, behind=0):
    vmem = pl.BlockSpec(memory_space=pltpu.VMEM)
    anywhere = pl.BlockSpec(memory_space=pl.ANY)
    return pl.pallas_call(
        kernel,
        out_shape=out_shape,
        in_specs=[vmem] * (len(args) - behind) + [anywhere] * behind,
        out_specs=(vmem,) * len(out_shape) if isinstance(out_shape, tuple) else vmem,
        scratch_shapes=list(scratch),
        compiler_params=pltpu.CompilerParams(vmem_limit_bytes=mib * 1024 * 1024),
        cost_estimate=pl.CostEstimate(flops=flops, bytes_accessed=0, transcendentals=0),
        name=name,
    )(*args)


def fast(hidden_acts, act_basis, out_grads, grad_basis, routed):
    scale = 1.0 / (hidden_acts.shape[0] * 16)
    slots = routed.reshape(8, 128)

    def sel(n):
        return pltpu.VMEM((n * SLOT, 1024), BF)

    def blk(dtype, *shape):
        return sds(shape[:-1] + (SLOT, shape[-1]), dtype)

    g_send = call(
        grads_send_kernel,
        "grads_send",
        blk(I16, 4, WIDTH),
        (slots, out_grads, grad_basis),
        (sel(4), pltpu.VMEM((4 * SLOT, WIDTH), F32)),
        flops=10_000_000_000,
    )
    g_got = lax.ppermute(g_send, "xl", SWAP)
    *z_send, x_send, z_keep, picked, bad = call(
        acts_send_kernel,
        "acts_send",
        (blk(I16, 2, AZ),) * 3
        + (blk(I16, 4, AX), blk(F32, 2, AZ), sds((8 * SLOT, hidden_acts.shape[1]), BF), sds((8, 128), F32)),
        (slots, hidden_acts, act_basis),
        (sel(8), pltpu.VMEM((8 * SLOT, AZ), F32)),
        24,
        4_000_000_000,
    )
    z_got = [lax.ppermute(s, "z", ring(d)) for s, d in zip(z_send, HOPS)]
    x_got = lax.ppermute(x_send, "xl", SWAP)
    g_keep = call(
        grads_keep_kernel,
        "grads_keep",
        sds((4 * SLOT, WIDTH), F32),
        (slots, out_grads, grad_basis, bad),
        (sel(4),),
        flops=600_000_000,
        behind=1,
    )
    x_keep = call(acts_keep_kernel, "acts_keep", sds((4 * SLOT, AX), F32), (picked, act_basis), flops=300_000_000)

    x_own, *x_next = call(
        x_mid_kernel,
        "x_mid",
        (blk(F32, WIDTH + AX),) + (blk(I16, WIDTH + AX),) * 3,
        (g_keep, g_got, x_keep, x_got),
        (pltpu.VMEM((3, SLOT, WIDTH + AX), F32),),
    )
    x_last = [lax.ppermute(s, "z", ring(d)) for s, d in zip(x_next, HOPS)]
    z_own, z_next = call(z_mid_kernel, "z_mid", (blk(F32, AZ), blk(I16, AZ)), (z_keep, *z_got, x_own), behind=1)
    z_last = lax.ppermute(z_next, "xl", SWAP)

    def gathered(rot):
        near = [rot] + [lax.ppermute(rot, "y", ring(d)) for d in HOPS]
        return near + [lax.ppermute(r, "core", SWAP) for r in near]

    rot_z = call(z_end_kernel, "z_end", blk(BF, AZ), (z_own, z_last))
    all_z = gathered(rot_z)
    rot_x = call(x_end_kernel, "x_end", blk(BF, WIDTH + AX), (x_own, *x_last, bad))
    all_x = gathered(rot_x)

    rows = pltpu.VMEM((GATHERED * PAD, WIDTH), BF)
    parts, whole = call(
        lambda *refs: gram_kernel(scale, *refs),
        "gram",
        (sds((16, 64, 384), BF), sds((8, 128), F32)),
        (*all_x, *all_z),
        (rows, rows),
        flops=600_000_000,
    )
    got = lax.all_to_all(parts, ("xh", "z", "xl"), 0, 0, tiled=True)
    return got, whole[0, 0] + lax.ppermute(whole, "xh", SWAP)[0, 0]


DP = ("y", "xh", "core")
TENSOR = ("z", "xl")


def general(hidden_acts, act_basis, out_grads, grad_basis, routed):
    act_part = jnp.dot(hidden_acts, act_basis, preferred_element_type=F32)
    grad_part = jnp.dot(out_grads, grad_basis, preferred_element_type=F32)
    act_sum, grad_sum = lax.psum((act_part, grad_part), TENSOR)
    rot_acts = act_sum.astype(BF)
    rot_grads = grad_sum.astype(BF)
    total_tokens = rot_acts.shape[0] * 16
    weights = routed.astype(F32)[:, None]
    acts_f = rot_acts.astype(F32)
    grads_f = rot_grads.astype(F32)
    masked_acts = (acts_f * weights).astype(BF)
    masked_grads = (grads_f * weights).astype(BF)
    sq_acts = (acts_f * acts_f * weights).astype(BF)
    sq_grads = (grads_f * grads_f).astype(BF)
    col_width = rot_acts.shape[1] // 8
    col_start = (lax.axis_index("z") * 2 + lax.axis_index("xl")) * col_width
    own_rows = rot_acts.shape[1] // 16
    row_start = ((lax.axis_index("y") * 2 + lax.axis_index("xh")) * 2 + lax.axis_index("core")) * own_rows
    contract = (((0,), (0,)), ((), ()))
    terms = []
    for left, right in ((masked_acts, rot_acts), (masked_grads, rot_grads), (sq_acts, sq_grads)):
        cols = lax.dynamic_slice_in_dim(right, col_start, col_width, 1)
        terms.append(lax.dot_general(left, cols, contract, preferred_element_type=F32))
    summed = lax.psum(jnp.concatenate(terms, axis=1) * (1.0 / total_tokens), DP)
    owned = lax.dynamic_slice_in_dim(summed, row_start, own_rows, 0)
    return tuple(owned[:, n * col_width : (n + 1) * col_width] for n in range(3))


def shards(*args):
    got, whole = fast(*args)

    def total(got, *_):
        return tuple(call(final_kernel, "final", (sds((64, 128), F32),) * 3, (got,)))

    return lax.cond(whole > 1.5, total, lambda _, *rest: general(*rest), got, *args)


def solution(mesh):
    fine = Mesh(mesh.devices.reshape(4, 2, 2, 4, 2), ("y", "xh", "core", "z", "xl"))
    return jax.shard_map(
        shards,
        mesh=fine,
        in_specs=(P(DP, TENSOR), P(TENSOR, None), P(DP, TENSOR), P(TENSOR, None), P(DP)),
        out_specs=(P(DP, TENSOR),) * 3,
        check_vma=False,
    )
```

```python
import jax
import jax.numpy as jnp
from jax import lax
from jax.experimental import pallas as pl
from jax.experimental.pallas import tpu as pltpu
from jax.sharding import Mesh
from jax.sharding import PartitionSpec as P

BF = jnp.bfloat16
F32 = jnp.float32
I16 = jnp.int16

SLOT = 72
KEEP = SLOT - 1
BLOCKS = 8
CAP = KEEP * BLOCKS
TOP = 32767.0
HOPS = (1, 3, 2)
ROUND = (2, 3, 1)


def ring(dist):
    return [(i, (i + dist) % 4) for i in range(4)]


SWAP = [(0, 1), (1, 0)]
WIDTH = 1024
AX = 256
AZ = WIDTH - AX


def last_row(shape):
    return lax.broadcasted_iota(jnp.int32, shape, len(shape) - 2) % SLOT == KEEP


def exponent_of(top):
    return jnp.clip(jnp.ceil(jnp.log2(jnp.maximum(top, 1e-37))), -100.0, 100.0)


def encode(x, k):
    y = x * jnp.exp2(-k)
    mag = jnp.abs(y)
    root = y * lax.rsqrt(jnp.maximum(mag, 1e-30))
    q = jnp.round(jnp.clip(root * TOP, -TOP, TOP))
    q = jnp.where(last_row(x.shape), k, q)
    return q.astype(jnp.int32).astype(I16)


def decode(q):
    q = q.astype(F32)
    unit = jnp.exp2(q[KEEP:SLOT, :]) * (1.0 / (TOP * TOP))
    x = q * jnp.abs(q) * unit
    return jnp.where(last_row(x.shape), 0.0, x)


def top_of(x):
    return jnp.max(jnp.max(jnp.abs(x), axis=1, keepdims=True), axis=0, keepdims=True)


def ranks(routed):
    r = routed.astype(F32).astype(BF)
    i = lax.broadcasted_iota(jnp.int32, (128, 128), 0)
    j = lax.broadcasted_iota(jnp.int32, (128, 128), 1)
    within = jnp.dot(r, (i <= j).astype(F32).astype(BF), preferred_element_type=F32)
    totals = jnp.dot(r, jnp.ones((128, 128), BF), preferred_element_type=F32)
    before = jnp.zeros((1, 128), F32)
    offs = []
    for row in range(8):
        offs.append(before)
        before = before + totals[row : row + 1, :]
    pos = within + jnp.concatenate(offs, axis=0) - 1.0
    return jnp.where(routed > 0, pos, -1.0), before


def build_select(sel_ref, pos, blocks):
    rows = len(blocks) * SLOT
    row = lax.broadcasted_iota(jnp.int32, (rows, 128), 0)
    base = jnp.zeros((rows, 128), jnp.int32)
    for b, q in enumerate(blocks):
        inside = (row >= b * SLOT) & (row < (b + 1) * SLOT)
        base = jnp.where(inside, q * KEEP - b * SLOT, base)
    want = jnp.where(row % SLOT == KEEP, -2, base + row).astype(F32)
    for c in range(8):
        sel_ref[:, c * 128 : (c + 1) * 128] = (want == pos[c : c + 1, :]).astype(F32).astype(BF)


def grads_send_kernel(routed_ref, g_ref, b_ref, send_ref, sel_ref, out_ref):
    z, xl = lax.axis_index("z"), lax.axis_index("xl")
    pos, _ = ranks(routed_ref[...])
    build_select(sel_ref, pos, [lax.rem(z + d, 4) * 2 + (1 - xl) for d in (0,) + HOPS])
    picked = jnp.dot(sel_ref[...], g_ref[...], preferred_element_type=F32).astype(BF)
    out_ref[...] = jnp.dot(picked, b_ref[...], preferred_element_type=F32)
    k = exponent_of(top_of(out_ref[...]))
    for b in range(4):
        send_ref[b] = encode(out_ref[b * SLOT : (b + 1) * SLOT, :], k)


def grads_keep_kernel(routed_ref, g_ref, b_ref, after_ref, keep_ref, sel_ref):
    z, xl = lax.axis_index("z"), lax.axis_index("xl")
    pos, _ = ranks(routed_ref[...])
    build_select(sel_ref, pos, [lax.rem(z + d, 4) * 2 + xl for d in (0,) + HOPS])
    picked = jnp.dot(sel_ref[...], g_ref[...], preferred_element_type=F32).astype(BF)
    keep_ref[...] = jnp.dot(picked, b_ref[...], preferred_element_type=F32)


def acts_z_kernel(routed_ref, h_ref, b_ref, s1_ref, s2_ref, s3_ref, picked_ref, bad_ref, sel_ref, z_ref):
    z, xl = lax.axis_index("z"), lax.axis_index("xl")
    pos, total = ranks(routed_ref[...])
    bad_ref[...] = jnp.broadcast_to(jnp.where(total > CAP, jnp.nan, 0.0), (8, 128))
    zs = [lax.rem(z + d, 4) * 2 for d in HOPS]
    build_select(sel_ref, pos, [zz + (1 - xl) for zz in zs] + [zz + xl for zz in zs])
    picked_ref[...] = jnp.dot(sel_ref[...], h_ref[...], preferred_element_type=F32).astype(BF)
    z_ref[...] = jnp.dot(picked_ref[...], b_ref[:, :AZ], preferred_element_type=F32)
    k = exponent_of(top_of(z_ref[...]))
    for n, s_ref in enumerate((s1_ref, s2_ref, s3_ref)):
        for b in range(2):
            at = (n + 3 * (1 - b)) * SLOT
            s_ref[b] = encode(z_ref[at : at + SLOT, :], k)


def acts_x_kernel(routed_ref, h_ref, b_ref, picked_ref, x_ref, near_ref, sel_ref):
    z, xl = lax.axis_index("z"), lax.axis_index("xl")
    pos, _ = ranks(routed_ref[...])
    build_select(sel_ref, pos, [z * 2 + (1 - xl), z * 2 + xl])
    near_ref[...] = jnp.dot(sel_ref[...], h_ref[...], preferred_element_type=F32).astype(BF)
    far = jnp.dot(picked_ref[: 3 * SLOT + 8, :], b_ref[:, AZ:], preferred_element_type=F32)
    near = jnp.dot(near_ref[: SLOT + 8, :], b_ref[:, AZ:], preferred_element_type=F32)
    parts = [near[:SLOT]] + [far[n * SLOT : (n + 1) * SLOT] for n in range(3)]
    top = top_of(parts[0])
    for part in parts[1:]:
        top = jnp.maximum(top, top_of(part))
    k = exponent_of(top)
    for b in range(4):
        x_ref[b] = encode(parts[b], k)


def acts_keep_kernel(picked_ref, near_ref, b_ref, z_ref, x_ref):
    far = jnp.dot(picked_ref[3 * SLOT - 8 :, :], b_ref[:, AZ:], preferred_element_type=F32)
    near = jnp.dot(near_ref[...], b_ref[...], preferred_element_type=F32)
    x_ref[:SLOT, :] = near[SLOT:, AZ:]
    x_ref[SLOT:, :] = far[8:, :]
    z_ref[0] = near[SLOT:, :AZ]
    z_ref[1] = near[:SLOT, :AZ]


def x_mid_kernel(g_keep, g_got, a_keep, a_got, own_ref, s1_ref, s2_ref, s3_ref, tmp_ref):
    def total(b):
        rows = slice(b * SLOT, (b + 1) * SLOT)
        return g_keep[rows, :] + decode(g_got[b]), a_keep[rows, :] + decode(a_got[b])

    g, a = total(0)
    own_ref[:, :WIDTH] = g
    own_ref[:, WIDTH:] = a
    top = jnp.zeros((1, 1), F32)
    for b in range(3):
        g, a = total(b + 1)
        tmp_ref[b, :, :WIDTH] = g
        tmp_ref[b, :, WIDTH:] = a
        top = jnp.maximum(top, jnp.maximum(top_of(g), top_of(a)))
    k = exponent_of(top)
    for b, s_ref in enumerate((s1_ref, s2_ref, s3_ref)):
        s_ref[...] = encode(tmp_ref[b], k)


def z_mid_kernel(keep_ref, r1_ref, r2_ref, r3_ref, after_ref, own_ref, send_ref):
    own_ref[...] = keep_ref[0] + decode(r1_ref[0]) + decode(r2_ref[0]) + decode(r3_ref[0])
    other = keep_ref[1] + decode(r1_ref[1]) + decode(r2_ref[1]) + decode(r3_ref[1])
    send_ref[...] = encode(other, exponent_of(top_of(other)))


def x_end_kernel(own_ref, r1_ref, r2_ref, r3_ref, bad_ref, rot_ref):
    x = own_ref[...] + decode(r1_ref[...]) + decode(r2_ref[...]) + decode(r3_ref[...])
    rot_ref[...] = (x + bad_ref[0:1, 0:1]).astype(BF)


def z_end_kernel(own_ref, got_ref, rot_ref):
    rot_ref[...] = (own_ref[...] + decode(got_ref[...])).astype(BF)


PAD = 80
GATHERED = 8
CONTRACT = (((0,), (0,)), ((), ()))


def gather_rows(dst_ref, cols, refs, part):
    for n, ref in enumerate(refs):
        dst_ref[n * PAD : n * PAD + SLOT, cols] = ref[:, part]
        dst_ref[n * PAD + SLOT : (n + 1) * PAD, cols] = jnp.zeros((PAD - SLOT, ref[:, part].shape[1]), BF)


def square(v):
    v = v.astype(F32)
    return (v * v).astype(BF)


def own_columns(x_ref):
    y, core = lax.axis_index("y"), lax.axis_index("core")
    i = lax.broadcasted_iota(jnp.int32, (256, 128), 0)
    j = lax.broadcasted_iota(jnp.int32, (256, 128), 1)
    pick = (i == j + jnp.where(j >= 64, 64, 0) + core * 64).astype(F32).astype(BF)
    x = x_ref[:, pl.ds(pl.multiple_of(y * 256, 256), 256)]
    return jnp.dot(x, pick, preferred_element_type=F32).astype(BF)


def put(out_ref, n, t):
    for xh in range(2):
        for cb in range(8):
            out_ref[xh * 8 + cb, :, n * 128 : (n + 1) * 128] = t[xh * 64 : (xh + 1) * 64, cb * 128 : (cb + 1) * 128]


def gram_kernel(scale, *refs):
    x_refs, z_refs = refs[:GATHERED], refs[GATHERED : 2 * GATHERED]
    out_ref, whole_ref, a_s, g_s = refs[2 * GATHERED :]
    marks = x_refs[0][0:8, 0:128].astype(F32)
    for ref in x_refs[1:]:
        marks = marks + ref[0:8, 0:128].astype(F32)
    whole_ref[...] = jnp.where(jnp.abs(marks) < 1e30, 1.0, 0.0)
    gather_rows(g_s, slice(0, WIDTH), x_refs, slice(0, WIDTH))
    gather_rows(a_s, slice(AZ, WIDTH), x_refs, slice(WIDTH, WIDTH + AX))
    gather_rows(a_s, slice(0, AZ), z_refs, slice(0, AZ))

    def dot(lhs, rhs):
        return (lax.dot_general(lhs, rhs, CONTRACT, preferred_element_type=F32) * scale).astype(BF)

    own = own_columns(a_s)
    put(out_ref, 1, dot(own_columns(g_s), g_s[...]))
    put(out_ref, 0, dot(own, a_s[...]))
    put(out_ref, 2, dot(square(own), square(g_s[...])))


def final_kernel(in_ref, a_ref, g_ref, c_ref):
    t = in_ref[0].astype(F32)
    for n in range(1, 16):
        t = t + in_ref[n].astype(F32)
    a_ref[...] = t[:, :128]
    g_ref[...] = t[:, 128:256]
    c_ref[...] = t[:, 256:]


def sds(shape, dtype):
    return jax.ShapeDtypeStruct(shape, dtype)


def call(kernel, name, out_shape, args, scratch=(), mib=16, flops=0, behind=0):
    vmem = pl.BlockSpec(memory_space=pltpu.VMEM)
    anywhere = pl.BlockSpec(memory_space=pl.ANY)
    return pl.pallas_call(
        kernel,
        out_shape=out_shape,
        in_specs=[vmem] * (len(args) - behind) + [anywhere] * behind,
        out_specs=(vmem,) * len(out_shape) if isinstance(out_shape, tuple) else vmem,
        scratch_shapes=list(scratch),
        compiler_params=pltpu.CompilerParams(vmem_limit_bytes=mib * 1024 * 1024),
        cost_estimate=pl.CostEstimate(flops=flops, bytes_accessed=0, transcendentals=0),
        name=name,
    )(*args)


def fast(hidden_acts, act_basis, out_grads, grad_basis, routed):
    scale = 1.0 / (hidden_acts.shape[0] * 16)
    slots = routed.reshape(8, 128)

    def sel(n):
        return pltpu.VMEM((n * SLOT, 1024), BF)

    def blk(dtype, *shape):
        return sds(shape[:-1] + (SLOT, shape[-1]), dtype)

    g_send = call(
        grads_send_kernel,
        "grads_send",
        blk(I16, 4, WIDTH),
        (slots, out_grads, grad_basis),
        (sel(4), pltpu.VMEM((4 * SLOT, WIDTH), F32)),
        flops=10_000_000_000,
    )
    g_got = lax.ppermute(g_send, "xl", SWAP)
    feats = hidden_acts.shape[1]
    *z_send, picked, bad = call(
        acts_z_kernel,
        "acts_z",
        (blk(I16, 2, AZ),) * 3 + (sds((6 * SLOT, feats), BF), sds((8, 128), F32)),
        (slots, hidden_acts, act_basis),
        (sel(6), pltpu.VMEM((6 * SLOT, AZ), F32)),
        24,
        4_000_000_000,
    )
    z_got = [lax.ppermute(s, "z", ring(d)) for s, d in zip(z_send, HOPS)]
    x_send, near = call(
        acts_x_kernel,
        "acts_x",
        (blk(I16, 4, AX), sds((2 * SLOT, feats), BF)),
        (slots, hidden_acts, act_basis, picked),
        (sel(2),),
        24,
        1_000_000_000,
    )
    x_got = lax.ppermute(x_send, "xl", SWAP)
    g_keep = call(
        grads_keep_kernel,
        "grads_keep",
        sds((4 * SLOT, WIDTH), F32),
        (slots, out_grads, grad_basis, near),
        (sel(4),),
        flops=600_000_000,
        behind=1,
    )
    z_keep, x_keep = call(
        acts_keep_kernel,
        "acts_keep",
        (blk(F32, 2, AZ), sds((4 * SLOT, AX), F32)),
        (picked, near, act_basis),
        flops=1_000_000_000,
    )

    x_own, *x_next = call(
        x_mid_kernel,
        "x_mid",
        (blk(F32, WIDTH + AX),) + (blk(I16, WIDTH + AX),) * 3,
        (g_keep, g_got, x_keep, x_got),
        (pltpu.VMEM((3, SLOT, WIDTH + AX), F32),),
    )
    x_last = [lax.ppermute(s, "z", ring(d)) for s, d in zip(x_next, HOPS)]
    z_own, z_next = call(z_mid_kernel, "z_mid", (blk(F32, AZ), blk(I16, AZ)), (z_keep, *z_got, x_own), behind=1)
    z_last = lax.ppermute(z_next, "xl", SWAP)

    def gathered(rot):
        near = [rot] + [lax.ppermute(rot, "y", ring(d)) for d in ROUND]
        return near + [lax.ppermute(r, "core", SWAP) for r in near]

    rot_z = call(z_end_kernel, "z_end", blk(BF, AZ), (z_own, z_last))
    all_z = gathered(rot_z)
    rot_x = call(x_end_kernel, "x_end", blk(BF, WIDTH + AX), (x_own, *x_last, bad))
    all_x = gathered(rot_x)

    rows = pltpu.VMEM((GATHERED * PAD, WIDTH), BF)
    parts, whole = call(
        lambda *refs: gram_kernel(scale, *refs),
        "gram",
        (sds((16, 64, 384), BF), sds((8, 128), F32)),
        (*all_x, *all_z),
        (rows, rows),
        flops=600_000_000,
    )
    got = lax.all_to_all(parts, ("xh", "z", "xl"), 0, 0, tiled=True)
    return got, whole[0, 0] + lax.ppermute(whole, "xh", SWAP)[0, 0]


DP = ("y", "xh", "core")
TENSOR = ("z", "xl")


def general(hidden_acts, act_basis, out_grads, grad_basis, routed):
    tokens, width = hidden_acts.shape[0], act_basis.shape[1]
    own = tokens // 8

    def rotated(values, basis):
        part = jnp.dot(values, basis, preferred_element_type=F32).reshape(8, own, width)
        return jnp.sum(lax.all_to_all(part, TENSOR, 0, 0, tiled=True), axis=0).astype(BF)

    def shared(left, right):
        term = lax.dot_general(left, right, CONTRACT, preferred_element_type=F32) * (1.0 / (tokens * 16))
        blocks = term.reshape(16, width // 16, 8, width // 8).transpose(0, 2, 1, 3).reshape(128, width // 16, width // 8)
        return jnp.sum(lax.all_to_all(blocks, DP + TENSOR, 0, 0, tiled=True), axis=0)

    place = lax.axis_index("z") * 2 + lax.axis_index("xl")
    weights = lax.dynamic_slice_in_dim(routed, place * own, own, 0).astype(F32)[:, None]
    rot_acts, rot_grads = rotated(hidden_acts, act_basis), rotated(out_grads, grad_basis)
    acts_f, grads_f = rot_acts.astype(F32), rot_grads.astype(F32)
    return (
        shared((acts_f * weights).astype(BF), rot_acts),
        shared((grads_f * weights).astype(BF), rot_grads),
        shared((acts_f * acts_f * weights).astype(BF), (grads_f * grads_f).astype(BF)),
    )


def shards(*args):
    got, whole = fast(*args)

    def total(got, *_):
        return tuple(call(final_kernel, "final", (sds((64, 128), F32),) * 3, (got,)))

    return lax.cond(whole > 1.5, total, lambda _, *rest: general(*rest), got, *args)


def solution(mesh):
    fine = Mesh(mesh.devices.reshape(4, 2, 2, 4, 2), ("y", "xh", "core", "z", "xl"))
    return jax.shard_map(
        shards,
        mesh=fine,
        in_specs=(P(DP, TENSOR), P(TENSOR, None), P(DP, TENSOR), P(TENSOR, None), P(DP)),
        out_specs=(P(DP, TENSOR),) * 3,
        check_vma=False,
    )
```

```python
import jax
import jax.numpy as jnp
from jax import lax
from jax.experimental import pallas as pl
from jax.experimental.pallas import tpu as pltpu
from jax.sharding import Mesh
from jax.sharding import PartitionSpec as P

BF = jnp.bfloat16
F32 = jnp.float32
I16 = jnp.int16

SLOT = 72
KEEP = SLOT - 1
BLOCKS = 8
CAP = KEEP * BLOCKS
TOP = 32767.0
HOPS = (1, 3, 2)
SIDES = [(2 * y + c, 2 * ((y + (-1) ** c) % 4) + c) for y in range(4) for c in range(2)]


def ring(dist):
    return [(i, (i + dist) % 4) for i in range(4)]


SWAP = [(0, 1), (1, 0)]
WIDTH = 1024
AX = 256
AZ = WIDTH - AX


def last_row(shape):
    return lax.broadcasted_iota(jnp.int32, shape, len(shape) - 2) % SLOT == KEEP


def exponent_of(top):
    return jnp.clip(jnp.ceil(jnp.log2(jnp.maximum(top, 1e-37))), -100.0, 100.0)


def encode(x, k):
    y = x * jnp.exp2(-k)
    mag = jnp.abs(y)
    root = y * lax.rsqrt(jnp.maximum(mag, 1e-30))
    q = jnp.round(jnp.clip(root * TOP, -TOP, TOP))
    q = jnp.where(last_row(x.shape), k, q)
    return q.astype(jnp.int32).astype(I16)


def decode(q):
    q = q.astype(F32)
    unit = jnp.exp2(q[KEEP:SLOT, :]) * (1.0 / (TOP * TOP))
    x = q * jnp.abs(q) * unit
    return jnp.where(last_row(x.shape), 0.0, x)


def top_of(x):
    return jnp.max(jnp.max(jnp.abs(x), axis=1, keepdims=True), axis=0, keepdims=True)


def ranks(routed):
    r = routed.astype(F32).astype(BF)
    i = lax.broadcasted_iota(jnp.int32, (128, 128), 0)
    j = lax.broadcasted_iota(jnp.int32, (128, 128), 1)
    within = jnp.dot(r, (i <= j).astype(F32).astype(BF), preferred_element_type=F32)
    totals = jnp.dot(r, jnp.ones((128, 128), BF), preferred_element_type=F32)
    before = jnp.zeros((1, 128), F32)
    offs = []
    for row in range(8):
        offs.append(before)
        before = before + totals[row : row + 1, :]
    pos = within + jnp.concatenate(offs, axis=0) - 1.0
    return jnp.where(routed > 0, pos, -1.0), before


def build_select(sel_ref, pos, blocks):
    rows = len(blocks) * SLOT
    row = lax.broadcasted_iota(jnp.int32, (rows, 128), 0)
    base = jnp.zeros((rows, 128), jnp.int32)
    for b, q in enumerate(blocks):
        inside = (row >= b * SLOT) & (row < (b + 1) * SLOT)
        base = jnp.where(inside, q * KEEP - b * SLOT, base)
    want = jnp.where(row % SLOT == KEEP, -2, base + row).astype(F32)
    for c in range(8):
        sel_ref[:, c * 128 : (c + 1) * 128] = (want == pos[c : c + 1, :]).astype(F32).astype(BF)


def grads_send_kernel(routed_ref, g_ref, b_ref, send_ref, sel_ref, out_ref):
    z, xl = lax.axis_index("z"), lax.axis_index("xl")
    pos, _ = ranks(routed_ref[...])
    build_select(sel_ref, pos, [lax.rem(z + d, 4) * 2 + (1 - xl) for d in (0,) + HOPS])
    picked = jnp.dot(sel_ref[...], g_ref[...], preferred_element_type=F32).astype(BF)
    out_ref[...] = jnp.dot(picked, b_ref[...], preferred_element_type=F32)
    k = exponent_of(top_of(out_ref[...]))
    for b in range(4):
        send_ref[b] = encode(out_ref[b * SLOT : (b + 1) * SLOT, :], k)


def grads_keep_kernel(routed_ref, g_ref, b_ref, after_ref, keep_ref, sel_ref):
    z, xl = lax.axis_index("z"), lax.axis_index("xl")
    pos, _ = ranks(routed_ref[...])
    build_select(sel_ref, pos, [lax.rem(z + d, 4) * 2 + xl for d in (0,) + HOPS])
    picked = jnp.dot(sel_ref[...], g_ref[...], preferred_element_type=F32).astype(BF)
    keep_ref[...] = jnp.dot(picked, b_ref[...], preferred_element_type=F32)


def acts_z_kernel(routed_ref, h_ref, b_ref, s1_ref, s2_ref, s3_ref, picked_ref, bad_ref, sel_ref, z_ref):
    z, xl = lax.axis_index("z"), lax.axis_index("xl")
    pos, total = ranks(routed_ref[...])
    bad_ref[...] = jnp.broadcast_to(jnp.where(total > CAP, jnp.nan, 0.0), (8, 128))
    zs = [lax.rem(z + d, 4) * 2 for d in HOPS]
    build_select(sel_ref, pos, [zz + (1 - xl) for zz in zs] + [zz + xl for zz in zs])
    picked_ref[...] = jnp.dot(sel_ref[...], h_ref[...], preferred_element_type=F32).astype(BF)
    z_ref[...] = jnp.dot(picked_ref[...], b_ref[:, :AZ], preferred_element_type=F32)
    k = exponent_of(top_of(z_ref[...]))
    for n, s_ref in enumerate((s1_ref, s2_ref, s3_ref)):
        for b in range(2):
            at = (n + 3 * (1 - b)) * SLOT
            s_ref[b] = encode(z_ref[at : at + SLOT, :], k)


def acts_x_kernel(routed_ref, h_ref, b_ref, picked_ref, x_ref, near_ref, sel_ref):
    z, xl = lax.axis_index("z"), lax.axis_index("xl")
    pos, _ = ranks(routed_ref[...])
    build_select(sel_ref, pos, [z * 2 + (1 - xl), z * 2 + xl])
    near_ref[...] = jnp.dot(sel_ref[...], h_ref[...], preferred_element_type=F32).astype(BF)
    far = jnp.dot(picked_ref[: 3 * SLOT + 8, :], b_ref[:, AZ:], preferred_element_type=F32)
    near = jnp.dot(near_ref[: SLOT + 8, :], b_ref[:, AZ:], preferred_element_type=F32)
    parts = [near[:SLOT]] + [far[n * SLOT : (n + 1) * SLOT] for n in range(3)]
    top = top_of(parts[0])
    for part in parts[1:]:
        top = jnp.maximum(top, top_of(part))
    k = exponent_of(top)
    for b in range(4):
        x_ref[b] = encode(parts[b], k)


def acts_keep_kernel(picked_ref, near_ref, b_ref, z_ref, x_ref):
    far = jnp.dot(picked_ref[3 * SLOT - 8 :, :], b_ref[:, AZ:], preferred_element_type=F32)
    near = jnp.dot(near_ref[...], b_ref[...], preferred_element_type=F32)
    x_ref[:SLOT, :] = near[SLOT:, AZ:]
    x_ref[SLOT:, :] = far[8:, :]
    z_ref[0] = near[SLOT:, :AZ]
    z_ref[1] = near[:SLOT, :AZ]


def x_mid_kernel(g_keep, g_got, a_keep, a_got, own_ref, s1_ref, s2_ref, s3_ref, tmp_ref):
    def total(b):
        rows = slice(b * SLOT, (b + 1) * SLOT)
        return g_keep[rows, :] + decode(g_got[b]), a_keep[rows, :] + decode(a_got[b])

    g, a = total(0)
    own_ref[:, :WIDTH] = g
    own_ref[:, WIDTH:] = a
    top = jnp.zeros((1, 1), F32)
    for b in range(3):
        g, a = total(b + 1)
        tmp_ref[b, :, :WIDTH] = g
        tmp_ref[b, :, WIDTH:] = a
        top = jnp.maximum(top, jnp.maximum(top_of(g), top_of(a)))
    k = exponent_of(top)
    for b, s_ref in enumerate((s1_ref, s2_ref, s3_ref)):
        s_ref[...] = encode(tmp_ref[b], k)


def z_mid_kernel(keep_ref, r1_ref, r2_ref, r3_ref, after_ref, own_ref, send_ref):
    own_ref[...] = keep_ref[0] + decode(r1_ref[0]) + decode(r2_ref[0]) + decode(r3_ref[0])
    other = keep_ref[1] + decode(r1_ref[1]) + decode(r2_ref[1]) + decode(r3_ref[1])
    send_ref[...] = encode(other, exponent_of(top_of(other)))


def x_end_kernel(own_ref, r1_ref, r2_ref, r3_ref, bad_ref, rot_ref):
    x = own_ref[...] + decode(r1_ref[...]) + decode(r2_ref[...]) + decode(r3_ref[...])
    rot_ref[...] = (x + bad_ref[0:1, 0:1]).astype(BF)


def z_end_kernel(own_ref, got_ref, rot_ref):
    rot_ref[...] = (own_ref[...] + decode(got_ref[...])).astype(BF)


PAD = 80
GATHERED = 8
CONTRACT = (((0,), (0,)), ((), ()))


def gather_rows(dst_ref, cols, blocks, part, places=range(GATHERED)):
    for n, block in zip(places, blocks):
        block = block[:, part]
        dst_ref[pl.ds(pl.multiple_of(n * PAD + PAD - 16, 16), 16), cols] = jnp.zeros((16, block.shape[1]), BF)
        dst_ref[pl.ds(pl.multiple_of(n * PAD, 16), SLOT), cols] = block


def both_kernel(own_ref, mate_ref, both_ref):
    both_ref[0] = own_ref[...]
    both_ref[1] = mate_ref[...]


def square(v):
    v = v.astype(F32)
    return (v * v).astype(BF)


def own_columns(x_ref):
    y, core = lax.axis_index("y"), lax.axis_index("core")
    i = lax.broadcasted_iota(jnp.int32, (256, 128), 0)
    j = lax.broadcasted_iota(jnp.int32, (256, 128), 1)
    pick = (i == j + jnp.where(j >= 64, 64, 0) + core * 64).astype(F32).astype(BF)
    x = x_ref[:, pl.ds(pl.multiple_of(y * 256, 256), 256)]
    return jnp.dot(x, pick, preferred_element_type=F32).astype(BF)


def put(out_ref, n, t):
    for xh in range(2):
        for cb in range(8):
            out_ref[xh * 8 + cb, :, n * 128 : (n + 1) * 128] = t[xh * 64 : (xh + 1) * 64, cb * 128 : (cb + 1) * 128]


def gram_kernel(scale, *refs):
    x_refs, z_refs = refs[:8], list(refs[8:12]) + [ref.at[n] for ref in refs[12:14] for n in range(2)]
    out_ref, whole_ref, a_s, g_s = refs[14:]
    core = lax.axis_index("core")
    places = (0, 1, 4 + 3 * core, 5 + core, 7 - 3 * core, 6 - core, 2, 3)
    marks = x_refs[0][0:8, 0:128].astype(F32)
    for ref in x_refs[1:]:
        marks = marks + ref[0:8, 0:128].astype(F32)
    whole_ref[...] = jnp.where(jnp.abs(marks) < 1e30, 1.0, 0.0)
    gather_rows(g_s, slice(0, WIDTH), x_refs, slice(0, WIDTH), places)
    gather_rows(a_s, slice(AZ, WIDTH), x_refs, slice(WIDTH, WIDTH + AX), places)
    gather_rows(a_s, slice(0, AZ), z_refs, slice(0, AZ))

    def dot(lhs, rhs):
        return (lax.dot_general(lhs, rhs, CONTRACT, preferred_element_type=F32) * scale).astype(BF)

    own = own_columns(a_s)
    put(out_ref, 1, dot(own_columns(g_s), g_s[...]))
    put(out_ref, 0, dot(own, a_s[...]))
    put(out_ref, 2, dot(square(own), square(g_s[...])))


def final_kernel(in_ref, a_ref, g_ref, c_ref):
    t = in_ref[0].astype(F32)
    for n in range(1, 16):
        t = t + in_ref[n].astype(F32)
    a_ref[...] = t[:, :128]
    g_ref[...] = t[:, 128:256]
    c_ref[...] = t[:, 256:]


def sds(shape, dtype):
    return jax.ShapeDtypeStruct(shape, dtype)


def call(kernel, name, out_shape, args, scratch=(), mib=16, flops=0, behind=0):
    vmem = pl.BlockSpec(memory_space=pltpu.VMEM)
    anywhere = pl.BlockSpec(memory_space=pl.ANY)
    return pl.pallas_call(
        kernel,
        out_shape=out_shape,
        in_specs=[vmem] * (len(args) - behind) + [anywhere] * behind,
        out_specs=(vmem,) * len(out_shape) if isinstance(out_shape, tuple) else vmem,
        scratch_shapes=list(scratch),
        compiler_params=pltpu.CompilerParams(vmem_limit_bytes=mib * 1024 * 1024),
        cost_estimate=pl.CostEstimate(flops=flops, bytes_accessed=0, transcendentals=0),
        name=name,
    )(*args)


def fast(hidden_acts, act_basis, out_grads, grad_basis, routed):
    scale = 1.0 / (hidden_acts.shape[0] * 16)
    slots = routed.reshape(8, 128)

    def sel(n):
        return pltpu.VMEM((n * SLOT, 1024), BF)

    def blk(dtype, *shape):
        return sds(shape[:-1] + (SLOT, shape[-1]), dtype)

    g_send = call(
        grads_send_kernel,
        "grads_send",
        blk(I16, 4, WIDTH),
        (slots, out_grads, grad_basis),
        (sel(4), pltpu.VMEM((4 * SLOT, WIDTH), F32)),
        flops=10_000_000_000,
    )
    g_got = lax.ppermute(g_send, "xl", SWAP)
    feats = hidden_acts.shape[1]
    *z_send, picked, bad = call(
        acts_z_kernel,
        "acts_z",
        (blk(I16, 2, AZ),) * 3 + (sds((6 * SLOT, feats), BF), sds((8, 128), F32)),
        (slots, hidden_acts, act_basis),
        (sel(6), pltpu.VMEM((6 * SLOT, AZ), F32)),
        24,
        4_000_000_000,
    )
    z_got = [lax.ppermute(s, "z", ring(d)) for s, d in zip(z_send, HOPS)]
    x_send, near = call(
        acts_x_kernel,
        "acts_x",
        (blk(I16, 4, AX), sds((2 * SLOT, feats), BF)),
        (slots, hidden_acts, act_basis, picked),
        (sel(2),),
        24,
        1_000_000_000,
    )
    x_got = lax.ppermute(x_send, "xl", SWAP)
    g_keep = call(
        grads_keep_kernel,
        "grads_keep",
        sds((4 * SLOT, WIDTH), F32),
        (slots, out_grads, grad_basis, near),
        (sel(4),),
        flops=600_000_000,
        behind=1,
    )
    z_keep, x_keep = call(
        acts_keep_kernel,
        "acts_keep",
        (blk(F32, 2, AZ), sds((4 * SLOT, AX), F32)),
        (picked, near, act_basis),
        flops=1_000_000_000,
    )

    x_own, *x_next = call(
        x_mid_kernel,
        "x_mid",
        (blk(F32, WIDTH + AX),) + (blk(I16, WIDTH + AX),) * 3,
        (g_keep, g_got, x_keep, x_got),
        (pltpu.VMEM((3, SLOT, WIDTH + AX), F32),),
    )
    x_last = [lax.ppermute(s, "z", ring(d)) for s, d in zip(x_next, HOPS)]
    z_own, z_next = call(z_mid_kernel, "z_mid", (blk(F32, AZ), blk(I16, AZ)), (z_keep, *z_got, x_own), behind=1)
    z_last = lax.ppermute(z_next, "xl", SWAP)

    def over(r):
        return lax.ppermute(r, "core", SWAP)

    rot_z = call(z_end_kernel, "z_end", blk(BF, AZ), (z_own, z_last))
    z_mate = over(rot_z)
    z_far = lax.ppermute(rot_z, "y", ring(2))
    z_both = call(both_kernel, "z_both", blk(BF, 2, AZ), (rot_z, z_mate))
    z_side = lax.ppermute(z_both, ("y", "core"), SIDES)
    all_z = (rot_z, z_mate, z_far, over(z_far), z_side, over(z_side))
    rot_x = call(x_end_kernel, "x_end", blk(BF, WIDTH + AX), (x_own, *x_last, bad))
    near = [rot_x] + [lax.ppermute(rot_x, "y", ring(d)) for d in (1, 3, 2)]
    all_x = [r for n in near for r in (n, over(n))]

    rows = pltpu.VMEM((GATHERED * PAD, WIDTH), BF)
    parts, whole = call(
        lambda *refs: gram_kernel(scale, *refs),
        "gram",
        (sds((16, 64, 384), BF), sds((8, 128), F32)),
        (*all_x, *all_z),
        (rows, rows),
        flops=600_000_000,
    )
    got = lax.all_to_all(parts, ("xh", "z", "xl"), 0, 0, tiled=True)
    return got, whole[0, 0] + lax.ppermute(whole, "xh", SWAP)[0, 0]


DP = ("y", "xh", "core")
TENSOR = ("z", "xl")


def general(hidden_acts, act_basis, out_grads, grad_basis, routed):
    tokens, width = hidden_acts.shape[0], act_basis.shape[1]
    own = tokens // 8

    def rotated(values, basis):
        part = jnp.dot(values, basis, preferred_element_type=F32).reshape(8, own, width)
        return jnp.sum(lax.all_to_all(part, TENSOR, 0, 0, tiled=True), axis=0).astype(BF)

    def shared(left, right):
        term = lax.dot_general(left, right, CONTRACT, preferred_element_type=F32) * (1.0 / (tokens * 16))
        blocks = term.reshape(16, width // 16, 8, width // 8).transpose(0, 2, 1, 3).reshape(128, width // 16, width // 8)
        return jnp.sum(lax.all_to_all(blocks, DP + TENSOR, 0, 0, tiled=True), axis=0)

    place = lax.axis_index("z") * 2 + lax.axis_index("xl")
    weights = lax.dynamic_slice_in_dim(routed, place * own, own, 0).astype(F32)[:, None]
    rot_acts, rot_grads = rotated(hidden_acts, act_basis), rotated(out_grads, grad_basis)
    acts_f, grads_f = rot_acts.astype(F32), rot_grads.astype(F32)
    return (
        shared((acts_f * weights).astype(BF), rot_acts),
        shared((grads_f * weights).astype(BF), rot_grads),
        shared((acts_f * acts_f * weights).astype(BF), (grads_f * grads_f).astype(BF)),
    )


def shards(*args):
    got, whole = fast(*args)

    def total(got, *_):
        return tuple(call(final_kernel, "final", (sds((64, 128), F32),) * 3, (got,)))

    return lax.cond(whole > 1.5, total, lambda _, *rest: general(*rest), got, *args)


def solution(mesh):
    fine = Mesh(mesh.devices.reshape(4, 2, 2, 4, 2), ("y", "xh", "core", "z", "xl"))
    return jax.shard_map(
        shards,
        mesh=fine,
        in_specs=(P(DP, TENSOR), P(TENSOR, None), P(DP, TENSOR), P(TENSOR, None), P(DP)),
        out_specs=(P(DP, TENSOR),) * 3,
        check_vma=False,
    )
```

```python
import jax
import jax.numpy as jnp
from jax import lax
from jax.experimental import pallas as pl
from jax.experimental.pallas import tpu as pltpu
from jax.sharding import Mesh
from jax.sharding import PartitionSpec as P

BF = jnp.bfloat16
F32 = jnp.float32
I16 = jnp.int16

SLOT = 72
KEEP = SLOT - 1
BLOCKS = 8
CAP = KEEP * BLOCKS
TOP = 32767.0
HOPS = (1, 3, 2)
SIDES = [(2 * y + c, 2 * ((y + (-1) ** c) % 4) + c) for y in range(4) for c in range(2)]


def ring(dist):
    return [(i, (i + dist) % 4) for i in range(4)]


SWAP = [(0, 1), (1, 0)]
WIDTH = 1024
AX = 256
AZ = WIDTH - AX


def last_row(shape):
    return lax.broadcasted_iota(jnp.int32, shape, len(shape) - 2) % SLOT == KEEP


def exponent_of(top):
    return jnp.clip(jnp.ceil(jnp.log2(jnp.maximum(top, 1e-37))), -100.0, 100.0)


def encode(x, k):
    y = x * jnp.exp2(-k)
    mag = jnp.abs(y)
    root = y * lax.rsqrt(jnp.maximum(mag, 1e-30))
    q = jnp.round(jnp.clip(root * TOP, -TOP, TOP))
    q = jnp.where(last_row(x.shape), k, q)
    return q.astype(jnp.int32).astype(I16)


def decode(q):
    q = q.astype(F32)
    unit = jnp.exp2(q[KEEP:SLOT, :]) * (1.0 / (TOP * TOP))
    x = q * jnp.abs(q) * unit
    return jnp.where(last_row(x.shape), 0.0, x)


def top_of(x):
    return jnp.max(jnp.max(jnp.abs(x), axis=1, keepdims=True), axis=0, keepdims=True)


def ranks(routed):
    r = routed.astype(F32).astype(BF)
    i = lax.broadcasted_iota(jnp.int32, (128, 128), 0)
    j = lax.broadcasted_iota(jnp.int32, (128, 128), 1)
    within = jnp.dot(r, (i <= j).astype(F32).astype(BF), preferred_element_type=F32)
    totals = jnp.dot(r, jnp.ones((128, 128), BF), preferred_element_type=F32)
    before = jnp.zeros((1, 128), F32)
    offs = []
    for row in range(8):
        offs.append(before)
        before = before + totals[row : row + 1, :]
    pos = within + jnp.concatenate(offs, axis=0) - 1.0
    return jnp.where(routed > 0, pos, -1.0), before


def build_select(sel_ref, pos, blocks):
    rows = len(blocks) * SLOT
    row = lax.broadcasted_iota(jnp.int32, (rows, 128), 0)
    base = jnp.zeros((rows, 128), jnp.int32)
    for b, q in enumerate(blocks):
        inside = (row >= b * SLOT) & (row < (b + 1) * SLOT)
        base = jnp.where(inside, q * KEEP - b * SLOT, base)
    want = jnp.where(row % SLOT == KEEP, -2, base + row).astype(F32)
    for c in range(8):
        sel_ref[:, c * 128 : (c + 1) * 128] = (want == pos[c : c + 1, :]).astype(F32).astype(BF)


def grads_send_kernel(routed_ref, g_ref, b_ref, send_ref, sel_ref, out_ref):
    z, xl = lax.axis_index("z"), lax.axis_index("xl")
    pos, _ = ranks(routed_ref[...])
    build_select(sel_ref, pos, [lax.rem(z + d, 4) * 2 + (1 - xl) for d in (0,) + HOPS])
    picked = jnp.dot(sel_ref[...], g_ref[...], preferred_element_type=F32).astype(BF)
    out_ref[...] = jnp.dot(picked, b_ref[...], preferred_element_type=F32)
    k = exponent_of(top_of(out_ref[...]))
    for b in range(4):
        send_ref[b] = encode(out_ref[b * SLOT : (b + 1) * SLOT, :], k)


def grads_keep_kernel(routed_ref, g_ref, b_ref, after_ref, keep_ref, sel_ref):
    z, xl = lax.axis_index("z"), lax.axis_index("xl")
    pos, _ = ranks(routed_ref[...])
    build_select(sel_ref, pos, [lax.rem(z + d, 4) * 2 + xl for d in (0,) + HOPS])
    picked = jnp.dot(sel_ref[...], g_ref[...], preferred_element_type=F32).astype(BF)
    keep_ref[...] = jnp.dot(picked, b_ref[...], preferred_element_type=F32)


def acts_z_kernel(routed_ref, h_ref, b_ref, s1_ref, s2_ref, s3_ref, picked_ref, bad_ref, sel_ref, z_ref):
    z, xl = lax.axis_index("z"), lax.axis_index("xl")
    pos, total = ranks(routed_ref[...])
    bad_ref[...] = jnp.broadcast_to(jnp.where(total > CAP, jnp.nan, 0.0), (8, 128))
    zs = [lax.rem(z + d, 4) * 2 for d in HOPS]
    build_select(sel_ref, pos, [zz + (1 - xl) for zz in zs] + [zz + xl for zz in zs])
    picked_ref[...] = jnp.dot(sel_ref[...], h_ref[...], preferred_element_type=F32).astype(BF)
    z_ref[...] = jnp.dot(picked_ref[...], b_ref[:, :AZ], preferred_element_type=F32)
    k = exponent_of(top_of(z_ref[...]))
    for n, s_ref in enumerate((s1_ref, s2_ref, s3_ref)):
        for b in range(2):
            at = (n + 3 * (1 - b)) * SLOT
            s_ref[b] = encode(z_ref[at : at + SLOT, :], k)


def acts_x_kernel(routed_ref, h_ref, b_ref, picked_ref, x_ref, near_ref, sel_ref):
    z, xl = lax.axis_index("z"), lax.axis_index("xl")
    pos, _ = ranks(routed_ref[...])
    build_select(sel_ref, pos, [z * 2 + (1 - xl), z * 2 + xl])
    near_ref[...] = jnp.dot(sel_ref[...], h_ref[...], preferred_element_type=F32).astype(BF)
    far = jnp.dot(picked_ref[: 3 * SLOT + 8, :], b_ref[:, AZ:], preferred_element_type=F32)
    near = jnp.dot(near_ref[: SLOT + 8, :], b_ref[:, AZ:], preferred_element_type=F32)
    parts = [near[:SLOT]] + [far[n * SLOT : (n + 1) * SLOT] for n in range(3)]
    top = top_of(parts[0])
    for part in parts[1:]:
        top = jnp.maximum(top, top_of(part))
    k = exponent_of(top)
    for b in range(4):
        x_ref[b] = encode(parts[b], k)


def acts_keep_kernel(picked_ref, near_ref, b_ref, z_ref, x_ref):
    far = jnp.dot(picked_ref[3 * SLOT - 8 :, :], b_ref[:, AZ:], preferred_element_type=F32)
    near = jnp.dot(near_ref[...], b_ref[...], preferred_element_type=F32)
    x_ref[:SLOT, :] = near[SLOT:, AZ:]
    x_ref[SLOT:, :] = far[8:, :]
    z_ref[0] = near[SLOT:, :AZ]
    z_ref[1] = near[:SLOT, :AZ]


def x_mid_kernel(g_keep, g_got, a_keep, a_got, own_ref, s1_ref, s2_ref, s3_ref, tmp_ref):
    def total(b):
        rows = slice(b * SLOT, (b + 1) * SLOT)
        return g_keep[rows, :] + decode(g_got[b]), a_keep[rows, :] + decode(a_got[b])

    g, a = total(0)
    own_ref[:, :WIDTH] = g
    own_ref[:, WIDTH:] = a
    top = jnp.zeros((1, 1), F32)
    for b in range(3):
        g, a = total(b + 1)
        tmp_ref[b, :, :WIDTH] = g
        tmp_ref[b, :, WIDTH:] = a
        top = jnp.maximum(top, jnp.maximum(top_of(g), top_of(a)))
    k = exponent_of(top)
    for b, s_ref in enumerate((s1_ref, s2_ref, s3_ref)):
        s_ref[...] = encode(tmp_ref[b], k)


def z_mid_kernel(keep_ref, r1_ref, r2_ref, r3_ref, after_ref, own_ref, send_ref):
    own_ref[...] = keep_ref[0] + decode(r1_ref[0]) + decode(r2_ref[0]) + decode(r3_ref[0])
    other = keep_ref[1] + decode(r1_ref[1]) + decode(r2_ref[1]) + decode(r3_ref[1])
    send_ref[...] = encode(other, exponent_of(top_of(other)))


def x_end_kernel(own_ref, r1_ref, r2_ref, r3_ref, bad_ref, rot_ref):
    x = own_ref[...] + decode(r1_ref[...]) + decode(r2_ref[...]) + decode(r3_ref[...])
    rot_ref[...] = (x + bad_ref[0:1, 0:1]).astype(BF)


def z_end_kernel(own_ref, got_ref, rot_ref):
    rot_ref[...] = (own_ref[...] + decode(got_ref[...])).astype(BF)


PAD = 80
GATHERED = 8
CONTRACT = (((0,), (0,)), ((), ()))


def gather_rows(dst_ref, cols, blocks, part, places=range(GATHERED)):
    for n, block in zip(places, blocks):
        block = block[:, part]
        dst_ref[pl.ds(pl.multiple_of(n * PAD + PAD - 16, 16), 16), cols] = jnp.zeros((16, block.shape[1]), BF)
        dst_ref[pl.ds(pl.multiple_of(n * PAD, 16), SLOT), cols] = block


def both_kernel(own_ref, mate_ref, both_ref):
    both_ref[0] = own_ref[...]
    both_ref[1] = mate_ref[...]


def square(v):
    v = v.astype(F32)
    return (v * v).astype(BF)


def own_columns(x_ref):
    y, core = lax.axis_index("y"), lax.axis_index("core")
    i = lax.broadcasted_iota(jnp.int32, (256, 128), 0)
    j = lax.broadcasted_iota(jnp.int32, (256, 128), 1)
    pick = (i == j + jnp.where(j >= 64, 64, 0) + core * 64).astype(F32).astype(BF)
    x = x_ref[:, pl.ds(pl.multiple_of(y * 256, 256), 256)]
    return jnp.dot(x, pick, preferred_element_type=F32).astype(BF)


def put(out_ref, n, t):
    for xh in range(2):
        for cb in range(8):
            out_ref[xh * 8 + cb, :, n * 128 : (n + 1) * 128] = t[xh * 64 : (xh + 1) * 64, cb * 128 : (cb + 1) * 128]


def gram_kernel(scale, *refs):
    x_refs, z_refs = refs[:8], list(refs[8:12]) + [ref.at[n] for ref in refs[12:14] for n in range(2)]
    out_ref, whole_ref, a_s, g_s = refs[14:]
    core = lax.axis_index("core")
    places = (0, 1, 4 + 3 * core, 5 + core, 7 - 3 * core, 6 - core, 2, 3)
    marks = x_refs[0][0:8, 0:128].astype(F32)
    for ref in x_refs[1:]:
        marks = marks + ref[0:8, 0:128].astype(F32)
    whole_ref[...] = jnp.where(jnp.abs(marks) < 1e30, 1.0, 0.0)
    gather_rows(g_s, slice(0, WIDTH), x_refs, slice(0, WIDTH), places)
    gather_rows(a_s, slice(AZ, WIDTH), x_refs, slice(WIDTH, WIDTH + AX), places)
    gather_rows(a_s, slice(0, AZ), z_refs, slice(0, AZ))

    def dot(lhs, rhs):
        return (lax.dot_general(lhs, rhs, CONTRACT, preferred_element_type=F32) * scale).astype(BF)

    own = own_columns(a_s)
    put(out_ref, 1, dot(own_columns(g_s), g_s[...]))
    put(out_ref, 0, dot(own, a_s[...]))
    put(out_ref, 2, dot(square(own), square(g_s[...])))


def final_kernel(in_ref, a_ref, g_ref, c_ref):
    t = in_ref[0].astype(F32)
    for n in range(1, 16):
        t = t + in_ref[n].astype(F32)
    a_ref[...] = t[:, :128]
    g_ref[...] = t[:, 128:256]
    c_ref[...] = t[:, 256:]


def sds(shape, dtype):
    return jax.ShapeDtypeStruct(shape, dtype)


def call(kernel, name, out_shape, args, scratch=(), mib=16, flops=0, behind=0):
    vmem = pl.BlockSpec(memory_space=pltpu.VMEM)
    anywhere = pl.BlockSpec(memory_space=pl.ANY)
    return pl.pallas_call(
        kernel,
        out_shape=out_shape,
        in_specs=[vmem] * (len(args) - behind) + [anywhere] * behind,
        out_specs=(vmem,) * len(out_shape) if isinstance(out_shape, tuple) else vmem,
        scratch_shapes=list(scratch),
        compiler_params=pltpu.CompilerParams(vmem_limit_bytes=mib * 1024 * 1024),
        cost_estimate=pl.CostEstimate(flops=flops, bytes_accessed=0, transcendentals=0),
        name=name,
    )(*args)


def fast(hidden_acts, act_basis, out_grads, grad_basis, routed):
    scale = 1.0 / (hidden_acts.shape[0] * 16)
    slots = routed.reshape(8, 128)

    def sel(n):
        return pltpu.VMEM((n * SLOT, 1024), BF)

    def blk(dtype, *shape):
        return sds(shape[:-1] + (SLOT, shape[-1]), dtype)

    g_send = call(
        grads_send_kernel,
        "grads_send",
        blk(I16, 4, WIDTH),
        (slots, out_grads, grad_basis),
        (sel(4), pltpu.VMEM((4 * SLOT, WIDTH), F32)),
        flops=10_000_000_000,
    )
    g_got = lax.ppermute(g_send, "xl", SWAP)
    feats = hidden_acts.shape[1]
    *z_send, picked, bad = call(
        acts_z_kernel,
        "acts_z",
        (blk(I16, 2, AZ),) * 3 + (sds((6 * SLOT, feats), BF), sds((8, 128), F32)),
        (slots, hidden_acts, act_basis),
        (sel(6), pltpu.VMEM((6 * SLOT, AZ), F32)),
        24,
        4_000_000_000,
    )
    z_got = [lax.ppermute(s, "z", ring(d)) for s, d in zip(z_send, HOPS)]
    x_send, near = call(
        acts_x_kernel,
        "acts_x",
        (blk(I16, 4, AX), sds((2 * SLOT, feats), BF)),
        (slots, hidden_acts, act_basis, picked),
        (sel(2),),
        24,
        1_000_000_000,
    )
    x_got = lax.ppermute(x_send, "xl", SWAP)
    g_keep = call(
        grads_keep_kernel,
        "grads_keep",
        sds((4 * SLOT, WIDTH), F32),
        (slots, out_grads, grad_basis, near),
        (sel(4),),
        flops=600_000_000,
        behind=1,
    )
    z_keep, x_keep = call(
        acts_keep_kernel,
        "acts_keep",
        (blk(F32, 2, AZ), sds((4 * SLOT, AX), F32)),
        (picked, near, act_basis),
        flops=1_000_000_000,
    )

    x_own, *x_next = call(
        x_mid_kernel,
        "x_mid",
        (blk(F32, WIDTH + AX),) + (blk(I16, WIDTH + AX),) * 3,
        (g_keep, g_got, x_keep, x_got),
        (pltpu.VMEM((3, SLOT, WIDTH + AX), F32),),
    )
    x_last = [lax.ppermute(s, "z", ring(d)) for s, d in zip(x_next, HOPS)]
    z_own, z_next = call(z_mid_kernel, "z_mid", (blk(F32, AZ), blk(I16, AZ)), (z_keep, *z_got, x_own), behind=1)
    z_last = lax.ppermute(z_next, "xl", SWAP)

    def over(r):
        return lax.ppermute(r, "core", SWAP)

    rot_z = call(z_end_kernel, "z_end", blk(BF, AZ), (z_own, z_last))
    z_mate = over(rot_z)
    z_far = lax.ppermute(rot_z, "y", ring(2))
    z_both = call(both_kernel, "z_both", blk(BF, 2, AZ), (rot_z, z_mate))
    z_side = lax.ppermute(z_both, ("y", "core"), SIDES)
    all_z = (rot_z, z_mate, z_far, over(z_far), z_side, over(z_side))
    rot_x = call(x_end_kernel, "x_end", blk(BF, WIDTH + AX), (x_own, *x_last, bad), flops=2_000_000_000)
    near = [rot_x] + [lax.ppermute(rot_x, "y", ring(d)) for d in (1, 3, 2)]
    all_x = [r for n in near for r in (n, over(n))]

    rows = pltpu.VMEM((GATHERED * PAD, WIDTH), BF)
    parts, whole = call(
        lambda *refs: gram_kernel(scale, *refs),
        "gram",
        (sds((16, 64, 384), BF), sds((8, 128), F32)),
        (*all_x, *all_z),
        (rows, rows),
        flops=600_000_000,
    )
    got = lax.all_to_all(parts, ("xh", "z", "xl"), 0, 0, tiled=True)
    return got, whole[0, 0] + lax.ppermute(whole, "xh", SWAP)[0, 0]


DP = ("y", "xh", "core")
TENSOR = ("z", "xl")


def general(hidden_acts, act_basis, out_grads, grad_basis, routed):
    tokens, width = hidden_acts.shape[0], act_basis.shape[1]
    own = tokens // 8

    def rotated(values, basis):
        part = jnp.dot(values, basis, preferred_element_type=F32).reshape(8, own, width)
        return jnp.sum(lax.all_to_all(part, TENSOR, 0, 0, tiled=True), axis=0).astype(BF)

    def shared(left, right):
        term = lax.dot_general(left, right, CONTRACT, preferred_element_type=F32) * (1.0 / (tokens * 16))
        blocks = term.reshape(16, width // 16, 8, width // 8).transpose(0, 2, 1, 3).reshape(128, width // 16, width // 8)
        return jnp.sum(lax.all_to_all(blocks, DP + TENSOR, 0, 0, tiled=True), axis=0)

    place = lax.axis_index("z") * 2 + lax.axis_index("xl")
    weights = lax.dynamic_slice_in_dim(routed, place * own, own, 0).astype(F32)[:, None]
    rot_acts, rot_grads = rotated(hidden_acts, act_basis), rotated(out_grads, grad_basis)
    acts_f, grads_f = rot_acts.astype(F32), rot_grads.astype(F32)
    return (
        shared((acts_f * weights).astype(BF), rot_acts),
        shared((grads_f * weights).astype(BF), rot_grads),
        shared((acts_f * acts_f * weights).astype(BF), (grads_f * grads_f).astype(BF)),
    )


def shards(*args):
    got, whole = fast(*args)

    def total(got, *_):
        return tuple(call(final_kernel, "final", (sds((64, 128), F32),) * 3, (got,)))

    return lax.cond(whole > 1.5, total, lambda _, *rest: general(*rest), got, *args)


def solution(mesh):
    fine = Mesh(mesh.devices.reshape(4, 2, 2, 4, 2), ("y", "xh", "core", "z", "xl"))
    return jax.shard_map(
        shards,
        mesh=fine,
        in_specs=(P(DP, TENSOR), P(TENSOR, None), P(DP, TENSOR), P(TENSOR, None), P(DP)),
        out_specs=(P(DP, TENSOR),) * 3,
        check_vma=False,
    )
```

```python
import jax
import jax.numpy as jnp
from jax import lax
from jax.experimental import pallas as pl
from jax.experimental.pallas import tpu as pltpu
from jax.sharding import Mesh
from jax.sharding import PartitionSpec as P

BF = jnp.bfloat16
F32 = jnp.float32
I16 = jnp.int16

SLOT = 72
KEEP = SLOT - 1
BLOCKS = 8
CAP = KEEP * BLOCKS
TOP = 32767.0
HOPS = (1, 3, 2)
SIDES = [(2 * y + c, 2 * ((y + (-1) ** c) % 4) + c) for y in range(4) for c in range(2)]


def ring(dist):
    return [(i, (i + dist) % 4) for i in range(4)]


SWAP = [(0, 1), (1, 0)]
WIDTH = 1024
AX = 256
AZ = WIDTH - AX


def last_row(shape):
    return lax.broadcasted_iota(jnp.int32, shape, len(shape) - 2) % SLOT == KEEP


def exponent_of(top):
    return jnp.clip(jnp.ceil(jnp.log2(jnp.maximum(top, 1e-37))), -100.0, 100.0)


def levels(x, k):
    y = x * jnp.exp2(-k)
    root = y * lax.rsqrt(jnp.maximum(jnp.abs(y), 1e-30))
    return jnp.round(jnp.clip(root * TOP, -TOP, TOP))


def values(q, k):
    return q * jnp.abs(q) * (jnp.exp2(k) * (1.0 / (TOP * TOP)))


def encode(x, k):
    return jnp.where(last_row(x.shape), k, levels(x, k)).astype(jnp.int32).astype(I16)


def decode(q):
    q = q.astype(F32)
    return jnp.where(last_row(q.shape), 0.0, values(q, q[KEEP:SLOT, :]))


def top_of(x):
    return jnp.max(jnp.max(jnp.abs(x), axis=1, keepdims=True), axis=0, keepdims=True)


def ranks(routed):
    r = routed.astype(F32).astype(BF)
    i = lax.broadcasted_iota(jnp.int32, (128, 128), 0)
    j = lax.broadcasted_iota(jnp.int32, (128, 128), 1)
    within = jnp.dot(r, (i <= j).astype(F32).astype(BF), preferred_element_type=F32)
    totals = jnp.dot(r, jnp.ones((128, 128), BF), preferred_element_type=F32)
    before = jnp.zeros((1, 128), F32)
    offs = []
    for row in range(8):
        offs.append(before)
        before = before + totals[row : row + 1, :]
    pos = within + jnp.concatenate(offs, axis=0) - 1.0
    return jnp.where(routed > 0, pos, -1.0), before


def build_select(sel_ref, pos, blocks):
    rows = len(blocks) * SLOT
    row = lax.broadcasted_iota(jnp.int32, (rows, 128), 0)
    base = jnp.zeros((rows, 128), jnp.int32)
    for b, q in enumerate(blocks):
        inside = (row >= b * SLOT) & (row < (b + 1) * SLOT)
        base = jnp.where(inside, q * KEEP - b * SLOT, base)
    want = jnp.where(row % SLOT == KEEP, -2, base + row).astype(F32)
    for c in range(8):
        sel_ref[:, c * 128 : (c + 1) * 128] = (want == pos[c : c + 1, :]).astype(F32).astype(BF)


def grads_send_kernel(routed_ref, g_ref, b_ref, send_ref, sel_ref, out_ref):
    z, xl = lax.axis_index("z"), lax.axis_index("xl")
    pos, _ = ranks(routed_ref[...])
    build_select(sel_ref, pos, [lax.rem(z + d, 4) * 2 + (1 - xl) for d in (0,) + HOPS])
    picked = jnp.dot(sel_ref[...], g_ref[...], preferred_element_type=F32).astype(BF)
    out_ref[...] = jnp.dot(picked, b_ref[...], preferred_element_type=F32)
    k = exponent_of(top_of(out_ref[...]))
    for b in range(4):
        send_ref[b] = encode(out_ref[b * SLOT : (b + 1) * SLOT, :], k)


def grads_keep_kernel(routed_ref, g_ref, b_ref, after_ref, keep_ref, sel_ref):
    z, xl = lax.axis_index("z"), lax.axis_index("xl")
    pos, _ = ranks(routed_ref[...])
    build_select(sel_ref, pos, [lax.rem(z + d, 4) * 2 + xl for d in (0,) + HOPS])
    picked = jnp.dot(sel_ref[...], g_ref[...], preferred_element_type=F32).astype(BF)
    keep_ref[...] = jnp.dot(picked, b_ref[...], preferred_element_type=F32)


def acts_z_kernel(routed_ref, h_ref, b_ref, s1_ref, s2_ref, s3_ref, picked_ref, bad_ref, sel_ref, z_ref):
    z, xl = lax.axis_index("z"), lax.axis_index("xl")
    pos, total = ranks(routed_ref[...])
    bad_ref[...] = jnp.broadcast_to(jnp.where(total > CAP, jnp.nan, 0.0), (8, 128))
    zs = [lax.rem(z + d, 4) * 2 for d in HOPS]
    build_select(sel_ref, pos, [zz + (1 - xl) for zz in zs] + [zz + xl for zz in zs])
    picked_ref[...] = jnp.dot(sel_ref[...], h_ref[...], preferred_element_type=F32).astype(BF)
    z_ref[...] = jnp.dot(picked_ref[...], b_ref[:, :AZ], preferred_element_type=F32)
    k = exponent_of(top_of(z_ref[...]))
    for n, s_ref in enumerate((s1_ref, s2_ref, s3_ref)):
        for b in range(2):
            at = (n + 3 * (1 - b)) * SLOT
            s_ref[b] = encode(z_ref[at : at + SLOT, :], k)


def acts_x_kernel(routed_ref, h_ref, b_ref, picked_ref, x_ref, near_ref, sel_ref):
    z, xl = lax.axis_index("z"), lax.axis_index("xl")
    pos, _ = ranks(routed_ref[...])
    build_select(sel_ref, pos, [z * 2 + (1 - xl), z * 2 + xl])
    near_ref[...] = jnp.dot(sel_ref[...], h_ref[...], preferred_element_type=F32).astype(BF)
    far = jnp.dot(picked_ref[: 3 * SLOT + 8, :], b_ref[:, AZ:], preferred_element_type=F32)
    near = jnp.dot(near_ref[: SLOT + 8, :], b_ref[:, AZ:], preferred_element_type=F32)
    parts = [near[:SLOT]] + [far[n * SLOT : (n + 1) * SLOT] for n in range(3)]
    top = top_of(parts[0])
    for part in parts[1:]:
        top = jnp.maximum(top, top_of(part))
    k = exponent_of(top)
    for b in range(4):
        x_ref[b] = encode(parts[b], k)


def acts_keep_kernel(picked_ref, near_ref, b_ref, z_ref, x_ref):
    far = jnp.dot(picked_ref[3 * SLOT - 8 :, :], b_ref[:, AZ:], preferred_element_type=F32)
    near = jnp.dot(near_ref[...], b_ref[...], preferred_element_type=F32)
    x_ref[:SLOT, :] = near[SLOT:, AZ:]
    x_ref[SLOT:, :] = far[8:, :]
    z_ref[0] = near[SLOT:, :AZ]
    z_ref[1] = near[:SLOT, :AZ]


def x_mid_kernel(g_keep, g_got, a_keep, a_got, own_ref, s1_ref, s2_ref, s3_ref, tmp_ref):
    def total(b):
        rows = slice(b * SLOT, (b + 1) * SLOT)
        return g_keep[rows, :] + decode(g_got[b]), a_keep[rows, :] + decode(a_got[b])

    g, a = total(0)
    own_ref[:, :WIDTH] = g
    own_ref[:, WIDTH:] = a
    top = jnp.zeros((1, 1), F32)
    for b in range(3):
        g, a = total(b + 1)
        tmp_ref[b, :, :WIDTH] = g
        tmp_ref[b, :, WIDTH:] = a
        top = jnp.maximum(top, jnp.maximum(top_of(g), top_of(a)))
    k = exponent_of(top)
    for b, s_ref in enumerate((s1_ref, s2_ref, s3_ref)):
        s_ref[...] = encode(tmp_ref[b], k)


def z_mid_kernel(keep_ref, r1_ref, r2_ref, r3_ref, after_ref, own_ref, send_ref):
    own_ref[...] = keep_ref[0] + decode(r1_ref[0]) + decode(r2_ref[0]) + decode(r3_ref[0])
    other = keep_ref[1] + decode(r1_ref[1]) + decode(r2_ref[1]) + decode(r3_ref[1])
    send_ref[...] = encode(other, exponent_of(top_of(other)))


def x_end_kernel(own_ref, r1_ref, r2_ref, r3_ref, bad_ref, rot_ref):
    x = own_ref[...] + decode(r1_ref[...]) + decode(r2_ref[...]) + decode(r3_ref[...])
    rot_ref[...] = (x + bad_ref[0:1, 0:1]).astype(BF)


def z_end_kernel(own_ref, got_ref, rot_ref):
    rot_ref[...] = (own_ref[...] + decode(got_ref[...])).astype(BF)


PAD = 80
GATHERED = 8
CONTRACT = (((0,), (0,)), ((), ()))


def gather_rows(dst_ref, cols, blocks, part, places=range(GATHERED)):
    for n, block in zip(places, blocks):
        block = block[:, part]
        dst_ref[pl.ds(pl.multiple_of(n * PAD + PAD - 16, 16), 16), cols] = jnp.zeros((16, block.shape[1]), BF)
        dst_ref[pl.ds(pl.multiple_of(n * PAD, 16), SLOT), cols] = block


def both_kernel(own_ref, mate_ref, both_ref):
    both_ref[0] = own_ref[...]
    both_ref[1] = mate_ref[...]


def square(v):
    v = v.astype(F32)
    return (v * v).astype(BF)


def own_columns(x_ref):
    y, core = lax.axis_index("y"), lax.axis_index("core")
    i = lax.broadcasted_iota(jnp.int32, (256, 128), 0)
    j = lax.broadcasted_iota(jnp.int32, (256, 128), 1)
    pick = (i == j + jnp.where(j >= 64, 64, 0) + core * 64).astype(F32).astype(BF)
    x = x_ref[:, pl.ds(pl.multiple_of(y * 256, 256), 256)]
    return jnp.dot(x, pick, preferred_element_type=F32).astype(BF)


def put(out_ref, n, t):
    cols = slice(n * 128, (n + 1) * 128)
    k = exponent_of(top_of(t))
    q = levels(t, k).astype(jnp.int32).astype(I16)
    for xh in range(2):
        for cb in range(8):
            out_ref[xh * 8 + cb, :64, cols] = q[xh * 64 : (xh + 1) * 64, cb * 128 : (cb + 1) * 128]
    scale = jnp.broadcast_to(k, (8, 128)).astype(jnp.int32).astype(I16)
    for n in range(16):
        out_ref[n, 64:, cols] = scale


def gram_kernel(scale, *refs):
    x_refs, z_refs = refs[:8], list(refs[8:12]) + [ref.at[n] for ref in refs[12:14] for n in range(2)]
    out_ref, whole_ref, a_s, g_s = refs[14:]
    core = lax.axis_index("core")
    places = (0, 1, 4 + 3 * core, 5 + core, 7 - 3 * core, 6 - core, 2, 3)
    marks = x_refs[0][0:8, 0:128].astype(F32)
    for ref in x_refs[1:]:
        marks = marks + ref[0:8, 0:128].astype(F32)
    whole_ref[...] = jnp.where(jnp.abs(marks) < 1e30, 1.0, 0.0)
    gather_rows(g_s, slice(0, WIDTH), x_refs, slice(0, WIDTH), places)
    gather_rows(a_s, slice(AZ, WIDTH), x_refs, slice(WIDTH, WIDTH + AX), places)
    gather_rows(a_s, slice(0, AZ), z_refs, slice(0, AZ))

    def dot(lhs, rhs):
        return lax.dot_general(lhs, rhs, CONTRACT, preferred_element_type=F32) * scale

    own = own_columns(a_s)
    put(out_ref, 1, dot(own_columns(g_s), g_s[...]))
    put(out_ref, 0, dot(own, a_s[...]))
    put(out_ref, 2, dot(square(own), square(g_s[...])))


def final_kernel(in_ref, a_ref, g_ref, c_ref):
    t = jnp.zeros((64, 384), F32)
    for n in range(16):
        t = t + values(in_ref[n, :64, :].astype(F32), in_ref[n, 64:, :].astype(F32)[:1, :])
    a_ref[...] = t[:, :128]
    g_ref[...] = t[:, 128:256]
    c_ref[...] = t[:, 256:]


def sds(shape, dtype):
    return jax.ShapeDtypeStruct(shape, dtype)


def call(kernel, name, out_shape, args, scratch=(), mib=16, flops=0, behind=0):
    vmem = pl.BlockSpec(memory_space=pltpu.VMEM)
    anywhere = pl.BlockSpec(memory_space=pl.ANY)
    return pl.pallas_call(
        kernel,
        out_shape=out_shape,
        in_specs=[vmem] * (len(args) - behind) + [anywhere] * behind,
        out_specs=(vmem,) * len(out_shape) if isinstance(out_shape, tuple) else vmem,
        scratch_shapes=list(scratch),
        compiler_params=pltpu.CompilerParams(vmem_limit_bytes=mib * 1024 * 1024),
        cost_estimate=pl.CostEstimate(flops=flops, bytes_accessed=0, transcendentals=0),
        name=name,
    )(*args)


def fast(hidden_acts, act_basis, out_grads, grad_basis, routed):
    scale = 1.0 / (hidden_acts.shape[0] * 16)
    slots = routed.reshape(8, 128)

    def sel(n):
        return pltpu.VMEM((n * SLOT, 1024), BF)

    def blk(dtype, *shape):
        return sds(shape[:-1] + (SLOT, shape[-1]), dtype)

    g_send = call(
        grads_send_kernel,
        "grads_send",
        blk(I16, 4, WIDTH),
        (slots, out_grads, grad_basis),
        (sel(4), pltpu.VMEM((4 * SLOT, WIDTH), F32)),
        flops=10_000_000_000,
    )
    g_got = lax.ppermute(g_send, "xl", SWAP)
    feats = hidden_acts.shape[1]
    *z_send, picked, bad = call(
        acts_z_kernel,
        "acts_z",
        (blk(I16, 2, AZ),) * 3 + (sds((6 * SLOT, feats), BF), sds((8, 128), F32)),
        (slots, hidden_acts, act_basis),
        (sel(6), pltpu.VMEM((6 * SLOT, AZ), F32)),
        24,
        4_000_000_000,
    )
    z_got = [lax.ppermute(s, "z", ring(d)) for s, d in zip(z_send, HOPS)]
    x_send, near = call(
        acts_x_kernel,
        "acts_x",
        (blk(I16, 4, AX), sds((2 * SLOT, feats), BF)),
        (slots, hidden_acts, act_basis, picked),
        (sel(2),),
        24,
        1_000_000_000,
    )
    x_got = lax.ppermute(x_send, "xl", SWAP)
    g_keep = call(
        grads_keep_kernel,
        "grads_keep",
        sds((4 * SLOT, WIDTH), F32),
        (slots, out_grads, grad_basis, near),
        (sel(4),),
        flops=600_000_000,
        behind=1,
    )
    z_keep, x_keep = call(
        acts_keep_kernel,
        "acts_keep",
        (blk(F32, 2, AZ), sds((4 * SLOT, AX), F32)),
        (picked, near, act_basis),
        flops=1_000_000_000,
    )

    x_own, *x_next = call(
        x_mid_kernel,
        "x_mid",
        (blk(F32, WIDTH + AX),) + (blk(I16, WIDTH + AX),) * 3,
        (g_keep, g_got, x_keep, x_got),
        (pltpu.VMEM((3, SLOT, WIDTH + AX), F32),),
    )
    x_last = [lax.ppermute(s, "z", ring(d)) for s, d in zip(x_next, HOPS)]
    z_own, z_next = call(z_mid_kernel, "z_mid", (blk(F32, AZ), blk(I16, AZ)), (z_keep, *z_got, x_own), behind=1)
    z_last = lax.ppermute(z_next, "xl", SWAP)

    def over(r):
        return lax.ppermute(r, "core", SWAP)

    rot_z = call(z_end_kernel, "z_end", blk(BF, AZ), (z_own, z_last))
    z_mate = over(rot_z)
    z_far = lax.ppermute(rot_z, "y", ring(2))
    z_both = call(both_kernel, "z_both", blk(BF, 2, AZ), (rot_z, z_mate))
    z_side = lax.ppermute(z_both, ("y", "core"), SIDES)
    all_z = (rot_z, z_mate, z_far, over(z_far), z_side, over(z_side))
    rot_x = call(x_end_kernel, "x_end", blk(BF, WIDTH + AX), (x_own, *x_last, bad), flops=2_000_000_000)
    near = [rot_x] + [lax.ppermute(rot_x, "y", ring(d)) for d in (1, 3, 2)]
    all_x = [r for n in near for r in (n, over(n))]

    rows = pltpu.VMEM((GATHERED * PAD, WIDTH), BF)
    parts, whole = call(
        lambda *refs: gram_kernel(scale, *refs),
        "gram",
        (sds((16, SLOT, 384), I16), sds((8, 128), F32)),
        (*all_x, *all_z),
        (rows, rows),
        flops=600_000_000,
    )
    got = lax.all_to_all(parts, ("xh", "z", "xl"), 0, 0, tiled=True)
    return got, whole[0, 0] + lax.ppermute(whole, "xh", SWAP)[0, 0]


DP = ("y", "xh", "core")
TENSOR = ("z", "xl")


def general(hidden_acts, act_basis, out_grads, grad_basis, routed):
    tokens, width = hidden_acts.shape[0], act_basis.shape[1]
    own = tokens // 8

    def rotated(values, basis):
        part = jnp.dot(values, basis, preferred_element_type=F32).reshape(8, own, width)
        return jnp.sum(lax.all_to_all(part, TENSOR, 0, 0, tiled=True), axis=0).astype(BF)

    def shared(left, right):
        term = lax.dot_general(left, right, CONTRACT, preferred_element_type=F32) * (1.0 / (tokens * 16))
        blocks = term.reshape(16, width // 16, 8, width // 8).transpose(0, 2, 1, 3).reshape(128, width // 16, width // 8)
        return jnp.sum(lax.all_to_all(blocks, DP + TENSOR, 0, 0, tiled=True), axis=0)

    place = lax.axis_index("z") * 2 + lax.axis_index("xl")
    weights = lax.dynamic_slice_in_dim(routed, place * own, own, 0).astype(F32)[:, None]
    rot_acts, rot_grads = rotated(hidden_acts, act_basis), rotated(out_grads, grad_basis)
    acts_f, grads_f = rot_acts.astype(F32), rot_grads.astype(F32)
    return (
        shared((acts_f * weights).astype(BF), rot_acts),
        shared((grads_f * weights).astype(BF), rot_grads),
        shared((acts_f * acts_f * weights).astype(BF), (grads_f * grads_f).astype(BF)),
    )


def shards(*args):
    got, whole = fast(*args)

    def total(got, *_):
        return tuple(call(final_kernel, "final", (sds((64, 128), F32),) * 3, (got,)))

    return lax.cond(whole > 1.5, total, lambda _, *rest: general(*rest), got, *args)


def solution(mesh):
    fine = Mesh(mesh.devices.reshape(4, 2, 2, 4, 2), ("y", "xh", "core", "z", "xl"))
    return jax.shard_map(
        shards,
        mesh=fine,
        in_specs=(P(DP, TENSOR), P(TENSOR, None), P(DP, TENSOR), P(TENSOR, None), P(DP)),
        out_specs=(P(DP, TENSOR),) * 3,
        check_vma=False,
    )
```

```python
import jax
import jax.numpy as jnp
from jax import lax
from jax.experimental import pallas as pl
from jax.experimental.pallas import tpu as pltpu
from jax.sharding import Mesh
from jax.sharding import PartitionSpec as P

BF = jnp.bfloat16
F32 = jnp.float32
I16 = jnp.int16

SLOT = 72
KEEP = SLOT - 1
BLOCKS = 8
CAP = KEEP * BLOCKS
FEW = 256
TOP = 32767.0
HOPS = (1, 3, 2)
SIDES = [(2 * y + c, 2 * ((y + (-1) ** c) % 4) + c) for y in range(4) for c in range(2)]


def ring(dist):
    return [(i, (i + dist) % 4) for i in range(4)]


SWAP = [(0, 1), (1, 0)]
WIDTH = 1024
AX = 256
AZ = WIDTH - AX


def last_row(shape):
    return lax.broadcasted_iota(jnp.int32, shape, len(shape) - 2) % SLOT == KEEP


def exponent_of(top):
    return jnp.clip(jnp.ceil(jnp.log2(jnp.maximum(top, 1e-37))), -100.0, 100.0)


def encode(x, k):
    y = x * jnp.exp2(-k)
    mag = jnp.abs(y)
    root = y * lax.rsqrt(jnp.maximum(mag, 1e-30))
    q = jnp.round(jnp.clip(root * TOP, -TOP, TOP))
    q = jnp.where(last_row(x.shape), k, q)
    return q.astype(jnp.int32).astype(I16)


def decode(q):
    q = q.astype(F32)
    unit = jnp.exp2(q[KEEP:SLOT, :]) * (1.0 / (TOP * TOP))
    x = q * jnp.abs(q) * unit
    return jnp.where(last_row(x.shape), 0.0, x)


def top_of(x):
    return jnp.max(jnp.max(jnp.abs(x), axis=1, keepdims=True), axis=0, keepdims=True)


def ranks(routed):
    r = routed.astype(F32).astype(BF)
    i = lax.broadcasted_iota(jnp.int32, (128, 128), 0)
    j = lax.broadcasted_iota(jnp.int32, (128, 128), 1)
    within = jnp.dot(r, (i <= j).astype(F32).astype(BF), preferred_element_type=F32)
    totals = jnp.dot(r, jnp.ones((128, 128), BF), preferred_element_type=F32)
    before = jnp.zeros((1, 128), F32)
    offs = []
    for row in range(8):
        offs.append(before)
        before = before + totals[row : row + 1, :]
    pos = within + jnp.concatenate(offs, axis=0) - 1.0
    return jnp.where(routed > 0, pos, -1.0), before


def build_select(sel_ref, pos, blocks):
    rows = len(blocks) * SLOT
    row = lax.broadcasted_iota(jnp.int32, (rows, 128), 0)
    base = jnp.zeros((rows, 128), jnp.int32)
    for b, q in enumerate(blocks):
        inside = (row >= b * SLOT) & (row < (b + 1) * SLOT)
        base = jnp.where(inside, q * KEEP - b * SLOT, base)
    want = jnp.where(row % SLOT == KEEP, -2, base + row).astype(F32)
    for c in range(8):
        sel_ref[:, c * 128 : (c + 1) * 128] = (want == pos[c : c + 1, :]).astype(F32).astype(BF)


def grads_send_kernel(routed_ref, g_ref, b_ref, send_ref, sel_ref, out_ref):
    z, xl = lax.axis_index("z"), lax.axis_index("xl")
    pos, _ = ranks(routed_ref[...])
    build_select(sel_ref, pos, [lax.rem(z + d, 4) * 2 + (1 - xl) for d in (0,) + HOPS])
    picked = jnp.dot(sel_ref[...], g_ref[...], preferred_element_type=F32).astype(BF)
    out_ref[...] = jnp.dot(picked, b_ref[...], preferred_element_type=F32)
    k = exponent_of(top_of(out_ref[...]))
    for b in range(4):
        send_ref[b] = encode(out_ref[b * SLOT : (b + 1) * SLOT, :], k)


def grads_keep_kernel(routed_ref, g_ref, b_ref, after_ref, keep_ref, sel_ref):
    z, xl = lax.axis_index("z"), lax.axis_index("xl")
    pos, _ = ranks(routed_ref[...])
    build_select(sel_ref, pos, [lax.rem(z + d, 4) * 2 + xl for d in (0,) + HOPS])
    picked = jnp.dot(sel_ref[...], g_ref[...], preferred_element_type=F32).astype(BF)
    keep_ref[...] = jnp.dot(picked, b_ref[...], preferred_element_type=F32)


def acts_z_kernel(routed_ref, h_ref, b_ref, s1_ref, s2_ref, s3_ref, picked_ref, bad_ref, sel_ref, z_ref):
    z, xl = lax.axis_index("z"), lax.axis_index("xl")
    pos, total = ranks(routed_ref[...])
    bad_ref[...] = jnp.broadcast_to(jnp.where((total > CAP) | (total < FEW), jnp.nan, 0.0), (8, 128))
    zs = [lax.rem(z + d, 4) * 2 for d in HOPS]
    build_select(sel_ref, pos, [zz + (1 - xl) for zz in zs] + [zz + xl for zz in zs])
    picked_ref[...] = jnp.dot(sel_ref[...], h_ref[...], preferred_element_type=F32).astype(BF)
    z_ref[...] = jnp.dot(picked_ref[...], b_ref[:, :AZ], preferred_element_type=F32)
    k = exponent_of(top_of(z_ref[...]))
    for n, s_ref in enumerate((s1_ref, s2_ref, s3_ref)):
        for b in range(2):
            at = (n + 3 * (1 - b)) * SLOT
            s_ref[b] = encode(z_ref[at : at + SLOT, :], k)


def acts_x_kernel(routed_ref, h_ref, b_ref, picked_ref, x_ref, near_ref, sel_ref):
    z, xl = lax.axis_index("z"), lax.axis_index("xl")
    pos, _ = ranks(routed_ref[...])
    build_select(sel_ref, pos, [z * 2 + (1 - xl), z * 2 + xl])
    near_ref[...] = jnp.dot(sel_ref[...], h_ref[...], preferred_element_type=F32).astype(BF)
    far = jnp.dot(picked_ref[: 3 * SLOT + 8, :], b_ref[:, AZ:], preferred_element_type=F32)
    near = jnp.dot(near_ref[: SLOT + 8, :], b_ref[:, AZ:], preferred_element_type=F32)
    parts = [near[:SLOT]] + [far[n * SLOT : (n + 1) * SLOT] for n in range(3)]
    top = top_of(parts[0])
    for part in parts[1:]:
        top = jnp.maximum(top, top_of(part))
    k = exponent_of(top)
    for b in range(4):
        x_ref[b] = encode(parts[b], k)


def acts_keep_kernel(picked_ref, near_ref, b_ref, z_ref, x_ref):
    far = jnp.dot(picked_ref[3 * SLOT - 8 :, :], b_ref[:, AZ:], preferred_element_type=F32)
    near = jnp.dot(near_ref[...], b_ref[...], preferred_element_type=F32)
    x_ref[:SLOT, :] = near[SLOT:, AZ:]
    x_ref[SLOT:, :] = far[8:, :]
    z_ref[0] = near[SLOT:, :AZ]
    z_ref[1] = near[:SLOT, :AZ]


def x_mid_kernel(g_keep, g_got, a_keep, a_got, own_ref, s1_ref, s2_ref, s3_ref, tmp_ref):
    def total(b):
        rows = slice(b * SLOT, (b + 1) * SLOT)
        return g_keep[rows, :] + decode(g_got[b]), a_keep[rows, :] + decode(a_got[b])

    g, a = total(0)
    own_ref[:, :WIDTH] = g
    own_ref[:, WIDTH:] = a
    top = jnp.zeros((1, 1), F32)
    for b in range(3):
        g, a = total(b + 1)
        tmp_ref[b, :, :WIDTH] = g
        tmp_ref[b, :, WIDTH:] = a
        top = jnp.maximum(top, jnp.maximum(top_of(g), top_of(a)))
    k = exponent_of(top)
    for b, s_ref in enumerate((s1_ref, s2_ref, s3_ref)):
        s_ref[...] = encode(tmp_ref[b], k)


def z_mid_kernel(keep_ref, r1_ref, r2_ref, r3_ref, after_ref, own_ref, send_ref):
    own_ref[...] = keep_ref[0] + decode(r1_ref[0]) + decode(r2_ref[0]) + decode(r3_ref[0])
    other = keep_ref[1] + decode(r1_ref[1]) + decode(r2_ref[1]) + decode(r3_ref[1])
    send_ref[...] = encode(other, exponent_of(top_of(other)))


def x_end_kernel(own_ref, r1_ref, r2_ref, r3_ref, bad_ref, rot_ref):
    x = own_ref[...] + decode(r1_ref[...]) + decode(r2_ref[...]) + decode(r3_ref[...])
    rot_ref[...] = (x + bad_ref[0:1, 0:1]).astype(BF)


def z_end_kernel(own_ref, got_ref, rot_ref):
    rot_ref[...] = (own_ref[...] + decode(got_ref[...])).astype(BF)


PAD = 80
GATHERED = 8
CONTRACT = (((0,), (0,)), ((), ()))


def gather_rows(dst_ref, cols, blocks, part, places=range(GATHERED)):
    for n, block in zip(places, blocks):
        block = block[:, part]
        dst_ref[pl.ds(pl.multiple_of(n * PAD + PAD - 16, 16), 16), cols] = jnp.zeros((16, block.shape[1]), BF)
        dst_ref[pl.ds(pl.multiple_of(n * PAD, 16), SLOT), cols] = block


def both_kernel(own_ref, mate_ref, both_ref):
    both_ref[0] = own_ref[...]
    both_ref[1] = mate_ref[...]


def square(v):
    v = v.astype(F32)
    return (v * v).astype(BF)


def own_columns(x_ref):
    y, core = lax.axis_index("y"), lax.axis_index("core")
    i = lax.broadcasted_iota(jnp.int32, (256, 128), 0)
    j = lax.broadcasted_iota(jnp.int32, (256, 128), 1)
    pick = (i == j + jnp.where(j >= 64, 64, 0) + core * 64).astype(F32).astype(BF)
    x = x_ref[:, pl.ds(pl.multiple_of(y * 256, 256), 256)]
    return jnp.dot(x, pick, preferred_element_type=F32).astype(BF)


def put(out_ref, n, t):
    for xh in range(2):
        for cb in range(8):
            out_ref[xh * 8 + cb, :, n * 128 : (n + 1) * 128] = t[xh * 64 : (xh + 1) * 64, cb * 128 : (cb + 1) * 128]


def gram_kernel(scale, *refs):
    x_refs, z_refs = refs[:8], list(refs[8:12]) + [ref.at[n] for ref in refs[12:14] for n in range(2)]
    out_ref, whole_ref, a_s, g_s = refs[14:]
    core = lax.axis_index("core")
    places = (0, 1, 4 + 3 * core, 5 + core, 7 - 3 * core, 6 - core, 2, 3)
    marks = x_refs[0][0:8, 0:128].astype(F32)
    for ref in x_refs[1:]:
        marks = marks + ref[0:8, 0:128].astype(F32)
    whole_ref[...] = jnp.where(jnp.abs(marks) < 1e30, 1.0, 0.0)
    gather_rows(g_s, slice(0, WIDTH), x_refs, slice(0, WIDTH), places)
    gather_rows(a_s, slice(AZ, WIDTH), x_refs, slice(WIDTH, WIDTH + AX), places)
    gather_rows(a_s, slice(0, AZ), z_refs, slice(0, AZ))

    def dot(lhs, rhs):
        return (lax.dot_general(lhs, rhs, CONTRACT, preferred_element_type=F32) * scale).astype(BF)

    own = own_columns(a_s)
    put(out_ref, 1, dot(own_columns(g_s), g_s[...]))
    put(out_ref, 0, dot(own, a_s[...]))
    put(out_ref, 2, dot(square(own), square(g_s[...])))


def final_kernel(in_ref, a_ref, g_ref, c_ref):
    t = in_ref[0].astype(F32)
    for n in range(1, 16):
        t = t + in_ref[n].astype(F32)
    a_ref[...] = t[:, :128]
    g_ref[...] = t[:, 128:256]
    c_ref[...] = t[:, 256:]


def sds(shape, dtype):
    return jax.ShapeDtypeStruct(shape, dtype)


def call(kernel, name, out_shape, args, scratch=(), mib=16, flops=0, behind=0):
    vmem = pl.BlockSpec(memory_space=pltpu.VMEM)
    anywhere = pl.BlockSpec(memory_space=pl.ANY)
    return pl.pallas_call(
        kernel,
        out_shape=out_shape,
        in_specs=[vmem] * (len(args) - behind) + [anywhere] * behind,
        out_specs=(vmem,) * len(out_shape) if isinstance(out_shape, tuple) else vmem,
        scratch_shapes=list(scratch),
        compiler_params=pltpu.CompilerParams(vmem_limit_bytes=mib * 1024 * 1024),
        cost_estimate=pl.CostEstimate(flops=flops, bytes_accessed=0, transcendentals=0),
        name=name,
    )(*args)


def fast(hidden_acts, act_basis, out_grads, grad_basis, routed):
    scale = 1.0 / (hidden_acts.shape[0] * 16)
    slots = routed.reshape(8, 128)

    def sel(n):
        return pltpu.VMEM((n * SLOT, 1024), BF)

    def blk(dtype, *shape):
        return sds(shape[:-1] + (SLOT, shape[-1]), dtype)

    g_send = call(
        grads_send_kernel,
        "grads_send",
        blk(I16, 4, WIDTH),
        (slots, out_grads, grad_basis),
        (sel(4), pltpu.VMEM((4 * SLOT, WIDTH), F32)),
        flops=10_000_000_000,
    )
    g_got = lax.ppermute(g_send, "xl", SWAP)
    feats = hidden_acts.shape[1]
    *z_send, picked, bad = call(
        acts_z_kernel,
        "acts_z",
        (blk(I16, 2, AZ),) * 3 + (sds((6 * SLOT, feats), BF), sds((8, 128), F32)),
        (slots, hidden_acts, act_basis),
        (sel(6), pltpu.VMEM((6 * SLOT, AZ), F32)),
        24,
        4_000_000_000,
    )
    z_got = [lax.ppermute(s, "z", ring(d)) for s, d in zip(z_send, HOPS)]
    x_send, near = call(
        acts_x_kernel,
        "acts_x",
        (blk(I16, 4, AX), sds((2 * SLOT, feats), BF)),
        (slots, hidden_acts, act_basis, picked),
        (sel(2),),
        24,
        1_000_000_000,
    )
    x_got = lax.ppermute(x_send, "xl", SWAP)
    g_keep = call(
        grads_keep_kernel,
        "grads_keep",
        sds((4 * SLOT, WIDTH), F32),
        (slots, out_grads, grad_basis, near),
        (sel(4),),
        flops=600_000_000,
        behind=1,
    )
    z_keep, x_keep = call(
        acts_keep_kernel,
        "acts_keep",
        (blk(F32, 2, AZ), sds((4 * SLOT, AX), F32)),
        (picked, near, act_basis),
        flops=1_000_000_000,
    )

    x_own, *x_next = call(
        x_mid_kernel,
        "x_mid",
        (blk(F32, WIDTH + AX),) + (blk(I16, WIDTH + AX),) * 3,
        (g_keep, g_got, x_keep, x_got),
        (pltpu.VMEM((3, SLOT, WIDTH + AX), F32),),
    )
    x_last = [lax.ppermute(s, "z", ring(d)) for s, d in zip(x_next, HOPS)]
    z_own, z_next = call(z_mid_kernel, "z_mid", (blk(F32, AZ), blk(I16, AZ)), (z_keep, *z_got, x_own), behind=1)
    z_last = lax.ppermute(z_next, "xl", SWAP)

    def over(r):
        return lax.ppermute(r, "core", SWAP)

    rot_z = call(z_end_kernel, "z_end", blk(BF, AZ), (z_own, z_last))
    z_mate = over(rot_z)
    z_far = lax.ppermute(rot_z, "y", ring(2))
    z_both = call(both_kernel, "z_both", blk(BF, 2, AZ), (rot_z, z_mate))
    z_side = lax.ppermute(z_both, ("y", "core"), SIDES)
    all_z = (rot_z, z_mate, z_far, over(z_far), z_side, over(z_side))
    rot_x = call(x_end_kernel, "x_end", blk(BF, WIDTH + AX), (x_own, *x_last, bad), flops=2_000_000_000)
    near = [rot_x] + [lax.ppermute(rot_x, "y", ring(d)) for d in (1, 3, 2)]
    all_x = [r for n in near for r in (n, over(n))]

    rows = pltpu.VMEM((GATHERED * PAD, WIDTH), BF)
    parts, whole = call(
        lambda *refs: gram_kernel(scale, *refs),
        "gram",
        (sds((16, 64, 384), BF), sds((8, 128), F32)),
        (*all_x, *all_z),
        (rows, rows),
        flops=600_000_000,
    )
    got = lax.all_to_all(parts, ("xh", "z", "xl"), 0, 0, tiled=True)
    return got, whole[0, 0] + lax.ppermute(whole, "xh", SWAP)[0, 0]


DP = ("y", "xh", "core")
TENSOR = ("z", "xl")


def general(hidden_acts, act_basis, out_grads, grad_basis, routed):
    tokens, width = hidden_acts.shape[0], act_basis.shape[1]
    own = tokens // 8

    def rotated(values, basis):
        part = jnp.dot(values, basis, preferred_element_type=F32).reshape(8, own, width)
        return jnp.sum(lax.all_to_all(part, TENSOR, 0, 0, tiled=True), axis=0).astype(BF)

    def shared(left, right):
        term = lax.dot_general(left, right, CONTRACT, preferred_element_type=F32) * (1.0 / (tokens * 16))
        blocks = term.reshape(16, width // 16, 8, width // 8).transpose(0, 2, 1, 3).reshape(128, width // 16, width // 8)
        return jnp.sum(lax.all_to_all(blocks, DP + TENSOR, 0, 0, tiled=True), axis=0)

    place = lax.axis_index("z") * 2 + lax.axis_index("xl")
    weights = lax.dynamic_slice_in_dim(routed, place * own, own, 0).astype(F32)[:, None]
    rot_acts, rot_grads = rotated(hidden_acts, act_basis), rotated(out_grads, grad_basis)
    acts_f, grads_f = rot_acts.astype(F32), rot_grads.astype(F32)
    return (
        shared((acts_f * weights).astype(BF), rot_acts),
        shared((grads_f * weights).astype(BF), rot_grads),
        shared((acts_f * acts_f * weights).astype(BF), (grads_f * grads_f).astype(BF)),
    )


def shards(*args):
    got, whole = fast(*args)

    def total(got, *_):
        return tuple(call(final_kernel, "final", (sds((64, 128), F32),) * 3, (got,)))

    return lax.cond(whole > 1.5, total, lambda _, *rest: general(*rest), got, *args)


def solution(mesh):
    fine = Mesh(mesh.devices.reshape(4, 2, 2, 4, 2), ("y", "xh", "core", "z", "xl"))
    return jax.shard_map(
        shards,
        mesh=fine,
        in_specs=(P(DP, TENSOR), P(TENSOR, None), P(DP, TENSOR), P(TENSOR, None), P(DP)),
        out_specs=(P(DP, TENSOR),) * 3,
        check_vma=False,
    )
```

```python
import jax
import jax.numpy as jnp
from jax import lax
from jax.experimental import pallas as pl
from jax.experimental.pallas import tpu as pltpu
from jax.sharding import Mesh
from jax.sharding import PartitionSpec as P

BF = jnp.bfloat16
F32 = jnp.float32
I16 = jnp.int16

SLOT = 72
KEEP = SLOT - 1
BLOCKS = 8
CAP = KEEP * BLOCKS
FEW = 256
TOP = 32767.0
HOPS = (1, 3, 2)
SIDES = [(2 * y + c, 2 * ((y + (-1) ** c) % 4) + c) for y in range(4) for c in range(2)]


def ring(dist):
    return [(i, (i + dist) % 4) for i in range(4)]


SWAP = [(0, 1), (1, 0)]
WIDTH = 1024
AX = 256
AZ = WIDTH - AX


def last_row(shape):
    return lax.broadcasted_iota(jnp.int32, shape, len(shape) - 2) % SLOT == KEEP


def exponent_of(top):
    return jnp.clip(jnp.ceil(jnp.log2(jnp.maximum(top, 1e-37))), -100.0, 100.0)


def encode(x, k):
    y = x * jnp.exp2(-k)
    mag = jnp.abs(y)
    root = y * lax.rsqrt(jnp.maximum(mag, 1e-30))
    q = jnp.round(jnp.clip(root * TOP, -TOP, TOP))
    q = jnp.where(last_row(x.shape), k, q)
    return q.astype(jnp.int32).astype(I16)


def decode(q):
    q = q.astype(F32)
    unit = jnp.exp2(q[KEEP:SLOT, :]) * (1.0 / (TOP * TOP))
    x = q * jnp.abs(q) * unit
    return jnp.where(last_row(x.shape), 0.0, x)


def top_of(x):
    return jnp.max(jnp.max(jnp.abs(x), axis=1, keepdims=True), axis=0, keepdims=True)


def ranks(routed):
    r = routed.astype(F32).astype(BF)
    i = lax.broadcasted_iota(jnp.int32, (128, 128), 0)
    j = lax.broadcasted_iota(jnp.int32, (128, 128), 1)
    within = jnp.dot(r, (i <= j).astype(F32).astype(BF), preferred_element_type=F32)
    totals = jnp.dot(r, jnp.ones((128, 128), BF), preferred_element_type=F32)
    before = jnp.zeros((1, 128), F32)
    offs = []
    for row in range(8):
        offs.append(before)
        before = before + totals[row : row + 1, :]
    pos = within + jnp.concatenate(offs, axis=0) - 1.0
    return jnp.where(routed > 0, pos, -1.0), before


def build_select(sel_ref, pos, blocks):
    rows = len(blocks) * SLOT
    row = lax.broadcasted_iota(jnp.int32, (rows, 128), 0)
    base = jnp.zeros((rows, 128), jnp.int32)
    for b, q in enumerate(blocks):
        inside = (row >= b * SLOT) & (row < (b + 1) * SLOT)
        base = jnp.where(inside, q * KEEP - b * SLOT, base)
    want = jnp.where(row % SLOT == KEEP, -2, base + row).astype(F32)
    for c in range(8):
        sel_ref[:, c * 128 : (c + 1) * 128] = (want == pos[c : c + 1, :]).astype(F32).astype(BF)


def grads_send_kernel(routed_ref, g_ref, b_ref, send_ref, sel_ref, out_ref):
    z, xl = lax.axis_index("z"), lax.axis_index("xl")
    pos, _ = ranks(routed_ref[...])
    build_select(sel_ref, pos, [lax.rem(z + d, 4) * 2 + (1 - xl) for d in (0,) + HOPS])
    picked = jnp.dot(sel_ref[...], g_ref[...], preferred_element_type=F32).astype(BF)
    out_ref[...] = jnp.dot(picked, b_ref[...], preferred_element_type=F32)
    k = exponent_of(top_of(out_ref[...]))
    for b in range(4):
        send_ref[b] = encode(out_ref[b * SLOT : (b + 1) * SLOT, :], k)


def grads_keep_kernel(routed_ref, g_ref, b_ref, after_ref, keep_ref, sel_ref):
    z, xl = lax.axis_index("z"), lax.axis_index("xl")
    pos, _ = ranks(routed_ref[...])
    build_select(sel_ref, pos, [lax.rem(z + d, 4) * 2 + xl for d in (0,) + HOPS])
    picked = jnp.dot(sel_ref[...], g_ref[...], preferred_element_type=F32).astype(BF)
    keep_ref[...] = jnp.dot(picked, b_ref[...], preferred_element_type=F32)


def acts_z_kernel(routed_ref, h_ref, b_ref, s1_ref, s2_ref, s3_ref, picked_ref, bad_ref, sel_ref, z_ref):
    z, xl = lax.axis_index("z"), lax.axis_index("xl")
    pos, total = ranks(routed_ref[...])
    bad_ref[...] = jnp.broadcast_to(jnp.where((total > CAP) | (total < FEW), jnp.nan, 0.0), (8, 128))
    zs = [lax.rem(z + d, 4) * 2 for d in HOPS]
    build_select(sel_ref, pos, [zz + (1 - xl) for zz in zs] + [zz + xl for zz in zs])
    picked_ref[...] = jnp.dot(sel_ref[...], h_ref[...], preferred_element_type=F32).astype(BF)
    z_ref[...] = jnp.dot(picked_ref[...], b_ref[:, :AZ], preferred_element_type=F32)
    k = exponent_of(top_of(z_ref[...]))
    for n, s_ref in enumerate((s1_ref, s2_ref, s3_ref)):
        for b in range(2):
            at = (n + 3 * (1 - b)) * SLOT
            s_ref[b] = encode(z_ref[at : at + SLOT, :], k)


def acts_x_kernel(routed_ref, h_ref, b_ref, picked_ref, x_ref, near_ref, sel_ref):
    z, xl = lax.axis_index("z"), lax.axis_index("xl")
    pos, _ = ranks(routed_ref[...])
    build_select(sel_ref, pos, [z * 2 + (1 - xl), z * 2 + xl])
    near_ref[...] = jnp.dot(sel_ref[...], h_ref[...], preferred_element_type=F32).astype(BF)
    far = jnp.dot(picked_ref[: 3 * SLOT + 8, :], b_ref[:, AZ:], preferred_element_type=F32)
    near = jnp.dot(near_ref[: SLOT + 8, :], b_ref[:, AZ:], preferred_element_type=F32)
    parts = [near[:SLOT]] + [far[n * SLOT : (n + 1) * SLOT] for n in range(3)]
    top = top_of(parts[0])
    for part in parts[1:]:
        top = jnp.maximum(top, top_of(part))
    k = exponent_of(top)
    for b in range(4):
        x_ref[b] = encode(parts[b], k)


def acts_keep_kernel(picked_ref, near_ref, b_ref, z_ref, x_ref):
    far = jnp.dot(picked_ref[3 * SLOT - 8 :, :], b_ref[:, AZ:], preferred_element_type=F32)
    near = jnp.dot(near_ref[...], b_ref[...], preferred_element_type=F32)
    x_ref[:SLOT, :] = near[SLOT:, AZ:]
    x_ref[SLOT:, :] = far[8:, :]
    z_ref[0] = near[SLOT:, :AZ]
    z_ref[1] = near[:SLOT, :AZ]


def x_mid_kernel(g_keep, g_got, a_keep, a_got, own_ref, s1_ref, s2_ref, s3_ref, tmp_ref):
    def total(b):
        rows = slice(b * SLOT, (b + 1) * SLOT)
        return g_keep[rows, :] + decode(g_got[b]), a_keep[rows, :] + decode(a_got[b])

    g, a = total(0)
    own_ref[:, :WIDTH] = g
    own_ref[:, WIDTH:] = a
    top = jnp.zeros((1, 1), F32)
    for b in range(3):
        g, a = total(b + 1)
        tmp_ref[b, :, :WIDTH] = g
        tmp_ref[b, :, WIDTH:] = a
        top = jnp.maximum(top, jnp.maximum(top_of(g), top_of(a)))
    k = exponent_of(top)
    for b, s_ref in enumerate((s1_ref, s2_ref, s3_ref)):
        s_ref[...] = encode(tmp_ref[b], k)


def z_mid_kernel(keep_ref, r1_ref, r2_ref, r3_ref, after_ref, own_ref, send_ref):
    own_ref[...] = keep_ref[0] + decode(r1_ref[0]) + decode(r2_ref[0]) + decode(r3_ref[0])
    other = keep_ref[1] + decode(r1_ref[1]) + decode(r2_ref[1]) + decode(r3_ref[1])
    send_ref[...] = encode(other, exponent_of(top_of(other)))


def x_end_kernel(own_ref, r1_ref, r2_ref, r3_ref, bad_ref, rot_ref):
    x = own_ref[...] + decode(r1_ref[...]) + decode(r2_ref[...]) + decode(r3_ref[...])
    rot_ref[...] = (x + bad_ref[0:1, 0:1]).astype(BF)


def z_end_kernel(own_ref, got_ref, rot_ref):
    rot_ref[...] = (own_ref[...] + decode(got_ref[...])).astype(BF)


PAD = 80
GATHERED = 8
CONTRACT = (((0,), (0,)), ((), ()))


def gather_rows(dst_ref, cols, blocks, part, places=range(GATHERED)):
    for n, block in zip(places, blocks):
        block = block[:, part]
        dst_ref[pl.ds(pl.multiple_of(n * PAD + PAD - 16, 16), 16), cols] = jnp.zeros((16, block.shape[1]), BF)
        dst_ref[pl.ds(pl.multiple_of(n * PAD, 16), SLOT), cols] = block


def both_kernel(own_ref, mate_ref, both_ref):
    both_ref[0] = own_ref[...]
    both_ref[1] = mate_ref[...]


def square(v):
    v = v.astype(F32)
    return (v * v).astype(BF)


def own_columns(x_ref):
    y, core = lax.axis_index("y"), lax.axis_index("core")
    i = lax.broadcasted_iota(jnp.int32, (256, 128), 0)
    j = lax.broadcasted_iota(jnp.int32, (256, 128), 1)
    pick = (i == j + jnp.where(j >= 64, 64, 0) + core * 64).astype(F32).astype(BF)
    x = x_ref[:, pl.ds(pl.multiple_of(y * 256, 256), 256)]
    return jnp.dot(x, pick, preferred_element_type=F32).astype(BF)


def put(out_ref, n, t):
    for xh in range(2):
        for cb in range(8):
            out_ref[xh * 8 + cb, :, n * 128 : (n + 1) * 128] = t[xh * 64 : (xh + 1) * 64, cb * 128 : (cb + 1) * 128]


def marks_of(x_refs):
    marks = x_refs[0][0:8, 0:128].astype(F32)
    for ref in x_refs[1:]:
        marks = marks + ref[0:8, 0:128].astype(F32)
    return marks


def terms(scale, a_s, g_s):
    own = own_columns(a_s)
    for lhs, rhs in ((own, a_s[...]), (own_columns(g_s), g_s[...]), (square(own), square(g_s[...]))):
        yield lax.dot_general(lhs, rhs, CONTRACT, preferred_element_type=F32) * scale


def near_kernel(scale, *refs):
    x_refs, z_refs = refs[:6], list(refs[6:8]) + [ref.at[n] for ref in refs[8:10] for n in range(2)]
    sum_ref, mark_ref, a_s, g_s = refs[10:]
    core = lax.axis_index("core")
    places = (0, 1, 2 + 3 * core, 3 + core, 5 - 3 * core, 4 - core)
    mark_ref[...] = marks_of(x_refs)
    gather_rows(g_s, slice(0, WIDTH), x_refs, slice(0, WIDTH), places)
    gather_rows(a_s, slice(AZ, WIDTH), x_refs, slice(WIDTH, WIDTH + AX), places)
    gather_rows(a_s, slice(0, AZ), z_refs, slice(0, AZ))
    for n, t in enumerate(terms(scale, a_s, g_s)):
        sum_ref[n] = t


def gram_kernel(scale, *refs):
    x_refs, z_refs, (sum_ref, mark_ref, out_ref, whole_ref, a_s, g_s) = refs[:2], refs[2:4], refs[4:]
    whole_ref[...] = jnp.where(jnp.abs(mark_ref[...] + marks_of(x_refs)) < 1e30, 1.0, 0.0)
    gather_rows(g_s, slice(0, WIDTH), x_refs, slice(0, WIDTH))
    gather_rows(a_s, slice(AZ, WIDTH), x_refs, slice(WIDTH, WIDTH + AX))
    gather_rows(a_s, slice(0, AZ), z_refs, slice(0, AZ))
    for n, t in enumerate(terms(scale, a_s, g_s)):
        put(out_ref, n, (sum_ref[n] + t).astype(BF))


def final_kernel(in_ref, a_ref, g_ref, c_ref):
    t = in_ref[0].astype(F32)
    for n in range(1, 16):
        t = t + in_ref[n].astype(F32)
    a_ref[...] = t[:, :128]
    g_ref[...] = t[:, 128:256]
    c_ref[...] = t[:, 256:]


def sds(shape, dtype):
    return jax.ShapeDtypeStruct(shape, dtype)


def call(kernel, name, out_shape, args, scratch=(), mib=16, flops=0, behind=0):
    vmem = pl.BlockSpec(memory_space=pltpu.VMEM)
    anywhere = pl.BlockSpec(memory_space=pl.ANY)
    return pl.pallas_call(
        kernel,
        out_shape=out_shape,
        in_specs=[vmem] * (len(args) - behind) + [anywhere] * behind,
        out_specs=(vmem,) * len(out_shape) if isinstance(out_shape, tuple) else vmem,
        scratch_shapes=list(scratch),
        compiler_params=pltpu.CompilerParams(vmem_limit_bytes=mib * 1024 * 1024),
        cost_estimate=pl.CostEstimate(flops=flops, bytes_accessed=0, transcendentals=0),
        name=name,
    )(*args)


def fast(hidden_acts, act_basis, out_grads, grad_basis, routed):
    scale = 1.0 / (hidden_acts.shape[0] * 16)
    slots = routed.reshape(8, 128)

    def sel(n):
        return pltpu.VMEM((n * SLOT, 1024), BF)

    def blk(dtype, *shape):
        return sds(shape[:-1] + (SLOT, shape[-1]), dtype)

    g_send = call(
        grads_send_kernel,
        "grads_send",
        blk(I16, 4, WIDTH),
        (slots, out_grads, grad_basis),
        (sel(4), pltpu.VMEM((4 * SLOT, WIDTH), F32)),
        flops=10_000_000_000,
    )
    g_got = lax.ppermute(g_send, "xl", SWAP)
    feats = hidden_acts.shape[1]
    *z_send, picked, bad = call(
        acts_z_kernel,
        "acts_z",
        (blk(I16, 2, AZ),) * 3 + (sds((6 * SLOT, feats), BF), sds((8, 128), F32)),
        (slots, hidden_acts, act_basis),
        (sel(6), pltpu.VMEM((6 * SLOT, AZ), F32)),
        24,
        4_000_000_000,
    )
    z_got = [lax.ppermute(s, "z", ring(d)) for s, d in zip(z_send, HOPS)]
    x_send, near = call(
        acts_x_kernel,
        "acts_x",
        (blk(I16, 4, AX), sds((2 * SLOT, feats), BF)),
        (slots, hidden_acts, act_basis, picked),
        (sel(2),),
        24,
        1_000_000_000,
    )
    x_got = lax.ppermute(x_send, "xl", SWAP)
    g_keep = call(
        grads_keep_kernel,
        "grads_keep",
        sds((4 * SLOT, WIDTH), F32),
        (slots, out_grads, grad_basis, near),
        (sel(4),),
        flops=600_000_000,
        behind=1,
    )
    z_keep, x_keep = call(
        acts_keep_kernel,
        "acts_keep",
        (blk(F32, 2, AZ), sds((4 * SLOT, AX), F32)),
        (picked, near, act_basis),
        flops=1_000_000_000,
    )

    x_own, *x_next = call(
        x_mid_kernel,
        "x_mid",
        (blk(F32, WIDTH + AX),) + (blk(I16, WIDTH + AX),) * 3,
        (g_keep, g_got, x_keep, x_got),
        (pltpu.VMEM((3, SLOT, WIDTH + AX), F32),),
    )
    x_last = [lax.ppermute(s, "z", ring(d)) for s, d in zip(x_next, HOPS)]
    z_own, z_next = call(z_mid_kernel, "z_mid", (blk(F32, AZ), blk(I16, AZ)), (z_keep, *z_got, x_own), behind=1)
    z_last = lax.ppermute(z_next, "xl", SWAP)

    def over(r):
        return lax.ppermute(r, "core", SWAP)

    rot_z = call(z_end_kernel, "z_end", blk(BF, AZ), (z_own, z_last))
    z_mate = over(rot_z)
    z_far = lax.ppermute(rot_z, "y", ring(2))
    z_both = call(both_kernel, "z_both", blk(BF, 2, AZ), (rot_z, z_mate))
    z_side = lax.ppermute(z_both, ("y", "core"), SIDES)
    all_z = (rot_z, z_mate, z_far, over(z_far), z_side, over(z_side))
    rot_x = call(x_end_kernel, "x_end", blk(BF, WIDTH + AX), (x_own, *x_last, bad), flops=2_000_000_000)
    near = [rot_x] + [lax.ppermute(rot_x, "y", ring(d)) for d in (1, 3, 2)]
    all_x = [r for n in near for r in (n, over(n))]

    def rows(n):
        return pltpu.VMEM((n * PAD, WIDTH), BF)

    sums, mark = call(
        lambda *refs: near_kernel(scale, *refs),
        "near",
        (sds((3, 128, WIDTH), F32), sds((8, 128), F32)),
        (*all_x[:6], *all_z[:2], *all_z[4:]),
        (rows(6), rows(6)),
        flops=500_000_000,
    )
    parts, whole = call(
        lambda *refs: gram_kernel(scale, *refs),
        "gram",
        (sds((16, 64, 384), BF), sds((8, 128), F32)),
        (*all_x[6:], *all_z[2:4], sums, mark),
        (rows(2), rows(2)),
        flops=200_000_000,
    )
    got = lax.all_to_all(parts, ("xh", "z", "xl"), 0, 0, tiled=True)
    return got, whole[0, 0] + lax.ppermute(whole, "xh", SWAP)[0, 0]


DP = ("y", "xh", "core")
TENSOR = ("z", "xl")


def general(hidden_acts, act_basis, out_grads, grad_basis, routed):
    tokens, width = hidden_acts.shape[0], act_basis.shape[1]
    own = tokens // 8

    def rotated(values, basis):
        part = jnp.dot(values, basis, preferred_element_type=F32).reshape(8, own, width)
        return jnp.sum(lax.all_to_all(part, TENSOR, 0, 0, tiled=True), axis=0).astype(BF)

    def shared(left, right):
        term = lax.dot_general(left, right, CONTRACT, preferred_element_type=F32) * (1.0 / (tokens * 16))
        blocks = term.reshape(16, width // 16, 8, width // 8).transpose(0, 2, 1, 3).reshape(128, width // 16, width // 8)
        return jnp.sum(lax.all_to_all(blocks, DP + TENSOR, 0, 0, tiled=True), axis=0)

    place = lax.axis_index("z") * 2 + lax.axis_index("xl")
    weights = lax.dynamic_slice_in_dim(routed, place * own, own, 0).astype(F32)[:, None]
    rot_acts, rot_grads = rotated(hidden_acts, act_basis), rotated(out_grads, grad_basis)
    acts_f, grads_f = rot_acts.astype(F32), rot_grads.astype(F32)
    return (
        shared((acts_f * weights).astype(BF), rot_acts),
        shared((grads_f * weights).astype(BF), rot_grads),
        shared((acts_f * acts_f * weights).astype(BF), (grads_f * grads_f).astype(BF)),
    )


def shards(*args):
    got, whole = fast(*args)

    def total(got, *_):
        return tuple(call(final_kernel, "final", (sds((64, 128), F32),) * 3, (got,)))

    return lax.cond(whole > 1.5, total, lambda _, *rest: general(*rest), got, *args)


def solution(mesh):
    fine = Mesh(mesh.devices.reshape(4, 2, 2, 4, 2), ("y", "xh", "core", "z", "xl"))
    return jax.shard_map(
        shards,
        mesh=fine,
        in_specs=(P(DP, TENSOR), P(TENSOR, None), P(DP, TENSOR), P(TENSOR, None), P(DP)),
        out_specs=(P(DP, TENSOR),) * 3,
        check_vma=False,
    )
```

```python
import jax
import jax.numpy as jnp
from jax import lax
from jax.experimental import pallas as pl
from jax.experimental.pallas import tpu as pltpu
from jax.sharding import Mesh
from jax.sharding import PartitionSpec as P

BF = jnp.bfloat16
F32 = jnp.float32
I16 = jnp.int16

SLOT = 72
KEEP = SLOT - 1
BLOCKS = 8
CAP = KEEP * BLOCKS
FEW = 256
TOP = 32767.0
HOPS = (1, 3, 2)
SIDES = [(2 * y + c, 2 * ((y + (-1) ** c) % 4) + c) for y in range(4) for c in range(2)]


def ring(dist):
    return [(i, (i + dist) % 4) for i in range(4)]


SWAP = [(0, 1), (1, 0)]
WIDTH = 1024
AX = 256
AZ = WIDTH - AX


def last_row(shape):
    return lax.broadcasted_iota(jnp.int32, shape, len(shape) - 2) % SLOT == KEEP


def exponent_of(top):
    return jnp.clip(jnp.ceil(jnp.log2(jnp.maximum(top, 1e-37))), -100.0, 100.0)


def encode(x, k):
    y = x * jnp.exp2(-k)
    mag = jnp.abs(y)
    root = y * lax.rsqrt(jnp.maximum(mag, 1e-30))
    q = jnp.round(jnp.clip(root * TOP, -TOP, TOP))
    q = jnp.where(last_row(x.shape), k, q)
    return q.astype(jnp.int32).astype(I16)


def decode(q):
    q = q.astype(F32)
    unit = jnp.exp2(q[KEEP:SLOT, :]) * (1.0 / (TOP * TOP))
    x = q * jnp.abs(q) * unit
    return jnp.where(last_row(x.shape), 0.0, x)


def top_of(x):
    return jnp.max(jnp.max(jnp.abs(x), axis=1, keepdims=True), axis=0, keepdims=True)


def ranks(routed):
    r = routed.astype(F32).astype(BF)
    i = lax.broadcasted_iota(jnp.int32, (128, 128), 0)
    j = lax.broadcasted_iota(jnp.int32, (128, 128), 1)
    within = jnp.dot(r, (i <= j).astype(F32).astype(BF), preferred_element_type=F32)
    totals = jnp.dot(r, jnp.ones((128, 128), BF), preferred_element_type=F32)
    before = jnp.zeros((1, 128), F32)
    offs = []
    for row in range(8):
        offs.append(before)
        before = before + totals[row : row + 1, :]
    pos = within + jnp.concatenate(offs, axis=0) - 1.0
    return jnp.where(routed > 0, pos, -1.0), before


def build_select(sel_ref, pos, blocks):
    rows = len(blocks) * SLOT
    row = lax.broadcasted_iota(jnp.int32, (rows, 128), 0)
    base = jnp.zeros((rows, 128), jnp.int32)
    for b, q in enumerate(blocks):
        inside = (row >= b * SLOT) & (row < (b + 1) * SLOT)
        base = jnp.where(inside, q * KEEP - b * SLOT, base)
    want = jnp.where(row % SLOT == KEEP, -2, base + row).astype(F32)
    for c in range(8):
        sel_ref[:, c * 128 : (c + 1) * 128] = (want == pos[c : c + 1, :]).astype(F32).astype(BF)


def grads_send_kernel(routed_ref, g_ref, b_ref, send_ref, sel_ref, out_ref):
    z, xl = lax.axis_index("z"), lax.axis_index("xl")
    pos, _ = ranks(routed_ref[...])
    build_select(sel_ref, pos, [lax.rem(z + d, 4) * 2 + (1 - xl) for d in (0,) + HOPS])
    picked = jnp.dot(sel_ref[...], g_ref[...], preferred_element_type=F32).astype(BF)
    out_ref[...] = jnp.dot(picked, b_ref[...], preferred_element_type=F32)
    k = exponent_of(top_of(out_ref[...]))
    for b in range(4):
        send_ref[b] = encode(out_ref[b * SLOT : (b + 1) * SLOT, :], k)


def grads_keep_kernel(routed_ref, g_ref, b_ref, after_ref, keep_ref, sel_ref):
    z, xl = lax.axis_index("z"), lax.axis_index("xl")
    pos, _ = ranks(routed_ref[...])
    build_select(sel_ref, pos, [lax.rem(z + d, 4) * 2 + xl for d in (0,) + HOPS])
    picked = jnp.dot(sel_ref[...], g_ref[...], preferred_element_type=F32).astype(BF)
    keep_ref[...] = jnp.dot(picked, b_ref[...], preferred_element_type=F32)


def acts_z_kernel(routed_ref, h_ref, b_ref, s1_ref, s2_ref, s3_ref, picked_ref, bad_ref, sel_ref, z_ref):
    z, xl = lax.axis_index("z"), lax.axis_index("xl")
    pos, total = ranks(routed_ref[...])
    bad_ref[...] = jnp.broadcast_to(jnp.where((total > CAP) | (total < FEW), jnp.nan, 0.0), (8, 128))
    zs = [lax.rem(z + d, 4) * 2 for d in HOPS]
    build_select(sel_ref, pos, [zz + (1 - xl) for zz in zs] + [zz + xl for zz in zs])
    picked_ref[...] = jnp.dot(sel_ref[...], h_ref[...], preferred_element_type=F32).astype(BF)
    z_ref[...] = jnp.dot(picked_ref[...], b_ref[:, :AZ], preferred_element_type=F32)
    k = exponent_of(top_of(z_ref[...]))
    for n, s_ref in enumerate((s1_ref, s2_ref, s3_ref)):
        for b in range(2):
            at = (n + 3 * (1 - b)) * SLOT
            s_ref[b] = encode(z_ref[at : at + SLOT, :], k)


def acts_x_kernel(routed_ref, h_ref, b_ref, picked_ref, x_ref, near_ref, sel_ref):
    z, xl = lax.axis_index("z"), lax.axis_index("xl")
    pos, _ = ranks(routed_ref[...])
    build_select(sel_ref, pos, [z * 2 + (1 - xl), z * 2 + xl])
    near_ref[...] = jnp.dot(sel_ref[...], h_ref[...], preferred_element_type=F32).astype(BF)
    far = jnp.dot(picked_ref[: 3 * SLOT + 8, :], b_ref[:, AZ:], preferred_element_type=F32)
    near = jnp.dot(near_ref[: SLOT + 8, :], b_ref[:, AZ:], preferred_element_type=F32)
    parts = [near[:SLOT]] + [far[n * SLOT : (n + 1) * SLOT] for n in range(3)]
    top = top_of(parts[0])
    for part in parts[1:]:
        top = jnp.maximum(top, top_of(part))
    k = exponent_of(top)
    for b in range(4):
        x_ref[b] = encode(parts[b], k)


def acts_keep_kernel(picked_ref, near_ref, b_ref, z_ref, x_ref):
    far = jnp.dot(picked_ref[3 * SLOT - 8 :, :], b_ref[:, AZ:], preferred_element_type=F32)
    near = jnp.dot(near_ref[...], b_ref[...], preferred_element_type=F32)
    x_ref[:SLOT, :] = near[SLOT:, AZ:]
    x_ref[SLOT:, :] = far[8:, :]
    z_ref[0] = near[SLOT:, :AZ]
    z_ref[1] = near[:SLOT, :AZ]


def x_mid_kernel(g_keep, g_got, a_keep, a_got, own_ref, s1_ref, s2_ref, s3_ref, tmp_ref):
    def total(b):
        rows = slice(b * SLOT, (b + 1) * SLOT)
        return g_keep[rows, :] + decode(g_got[b]), a_keep[rows, :] + decode(a_got[b])

    g, a = total(0)
    own_ref[:, :WIDTH] = g
    own_ref[:, WIDTH:] = a
    top = jnp.zeros((1, 1), F32)
    for b in range(3):
        g, a = total(b + 1)
        tmp_ref[b, :, :WIDTH] = g
        tmp_ref[b, :, WIDTH:] = a
        top = jnp.maximum(top, jnp.maximum(top_of(g), top_of(a)))
    k = exponent_of(top)
    for b, s_ref in enumerate((s1_ref, s2_ref, s3_ref)):
        s_ref[...] = encode(tmp_ref[b], k)


def z_mid_kernel(keep_ref, r1_ref, r2_ref, r3_ref, after_ref, own_ref, send_ref):
    own_ref[...] = keep_ref[0] + decode(r1_ref[0]) + decode(r2_ref[0]) + decode(r3_ref[0])
    other = keep_ref[1] + decode(r1_ref[1]) + decode(r2_ref[1]) + decode(r3_ref[1])
    send_ref[...] = encode(other, exponent_of(top_of(other)))


def x_end_kernel(own_ref, r1_ref, r2_ref, r3_ref, bad_ref, rot_ref):
    x = own_ref[...] + decode(r1_ref[...]) + decode(r2_ref[...]) + decode(r3_ref[...])
    rot_ref[...] = (x + bad_ref[0:1, 0:1]).astype(BF)


def z_end_kernel(own_ref, got_ref, rot_ref):
    rot_ref[...] = (own_ref[...] + decode(got_ref[...])).astype(BF)


PAD = 80
GATHERED = 8
CONTRACT = (((0,), (0,)), ((), ()))


def gather_rows(dst_ref, cols, blocks, part, places=range(GATHERED)):
    for n, block in zip(places, blocks):
        block = block[:, part]
        dst_ref[pl.ds(pl.multiple_of(n * PAD + PAD - 16, 16), 16), cols] = jnp.zeros((16, block.shape[1]), BF)
        dst_ref[pl.ds(pl.multiple_of(n * PAD, 16), SLOT), cols] = block


def both_kernel(own_ref, mate_ref, both_ref):
    both_ref[0] = own_ref[...]
    both_ref[1] = mate_ref[...]


def square(v):
    v = v.astype(F32)
    return (v * v).astype(BF)


def own_columns(x_ref):
    y, core = lax.axis_index("y"), lax.axis_index("core")
    i = lax.broadcasted_iota(jnp.int32, (256, 128), 0)
    j = lax.broadcasted_iota(jnp.int32, (256, 128), 1)
    pick = (i == j + jnp.where(j >= 64, 64, 0) + core * 64).astype(F32).astype(BF)
    x = x_ref[:, pl.ds(pl.multiple_of(y * 256, 256), 256)]
    return jnp.dot(x, pick, preferred_element_type=F32).astype(BF)


def put(out_ref, n, t):
    for xh in range(2):
        for cb in range(8):
            out_ref[xh * 8 + cb, :, n * 128 : (n + 1) * 128] = t[xh * 64 : (xh + 1) * 64, cb * 128 : (cb + 1) * 128]


def gram_kernel(scale, *refs):
    x_refs, z_refs = refs[:8], list(refs[8:12]) + [ref.at[n] for ref in refs[12:14] for n in range(2)]
    out_ref, whole_ref, a_s, g_s = refs[14:]
    core = lax.axis_index("core")
    places = (0, 1, 4 + 3 * core, 5 + core, 7 - 3 * core, 6 - core, 2, 3)
    marks = x_refs[0][0:8, 0:128].astype(F32)
    for ref in x_refs[1:]:
        marks = marks + ref[0:8, 0:128].astype(F32)
    whole_ref[...] = jnp.where(jnp.abs(marks) < 1e30, 1.0, 0.0)
    gather_rows(g_s, slice(0, WIDTH), x_refs, slice(0, WIDTH), places)
    gather_rows(a_s, slice(AZ, WIDTH), x_refs, slice(WIDTH, WIDTH + AX), places)
    gather_rows(a_s, slice(0, AZ), z_refs, slice(0, AZ))

    def dot(lhs, rhs):
        return (lax.dot_general(lhs, rhs, CONTRACT, preferred_element_type=F32) * scale).astype(BF)

    own = own_columns(a_s)
    put(out_ref, 1, dot(own_columns(g_s), g_s[...]))
    put(out_ref, 0, dot(own, a_s[...]))
    put(out_ref, 2, dot(square(own), square(g_s[...])))


def final_kernel(in_ref, a_ref, g_ref, c_ref):
    t = in_ref[0].astype(F32)
    for n in range(1, 16):
        t = t + in_ref[n].astype(F32)
    a_ref[...] = t[:, :128]
    g_ref[...] = t[:, 128:256]
    c_ref[...] = t[:, 256:]


def sds(shape, dtype):
    return jax.ShapeDtypeStruct(shape, dtype)


def call(kernel, name, out_shape, args, scratch=(), mib=16, flops=0, behind=0):
    vmem = pl.BlockSpec(memory_space=pltpu.VMEM)
    anywhere = pl.BlockSpec(memory_space=pl.ANY)
    return pl.pallas_call(
        kernel,
        out_shape=out_shape,
        in_specs=[vmem] * (len(args) - behind) + [anywhere] * behind,
        out_specs=(vmem,) * len(out_shape) if isinstance(out_shape, tuple) else vmem,
        scratch_shapes=list(scratch),
        compiler_params=pltpu.CompilerParams(vmem_limit_bytes=mib * 1024 * 1024),
        cost_estimate=pl.CostEstimate(flops=flops, bytes_accessed=0, transcendentals=0),
        name=name,
    )(*args)


def fast(hidden_acts, act_basis, out_grads, grad_basis, routed):
    scale = 1.0 / (hidden_acts.shape[0] * 16)
    slots = routed.reshape(8, 128)

    def sel(n):
        return pltpu.VMEM((n * SLOT, 1024), BF)

    def blk(dtype, *shape):
        return sds(shape[:-1] + (SLOT, shape[-1]), dtype)

    g_send = call(
        grads_send_kernel,
        "grads_send",
        blk(I16, 4, WIDTH),
        (slots, out_grads, grad_basis),
        (sel(4), pltpu.VMEM((4 * SLOT, WIDTH), F32)),
        flops=10_000_000_000,
    )
    g_got = lax.ppermute(g_send, "xl", SWAP)
    feats = hidden_acts.shape[1]
    *z_send, picked, bad = call(
        acts_z_kernel,
        "acts_z",
        (blk(I16, 2, AZ),) * 3 + (sds((6 * SLOT, feats), BF), sds((8, 128), F32)),
        (slots, hidden_acts, act_basis),
        (sel(6), pltpu.VMEM((6 * SLOT, AZ), F32)),
        24,
        4_000_000_000,
    )
    z_got = [lax.ppermute(s, "z", ring(d)) for s, d in zip(z_send, HOPS)]
    x_send, near = call(
        acts_x_kernel,
        "acts_x",
        (blk(I16, 4, AX), sds((2 * SLOT, feats), BF)),
        (slots, hidden_acts, act_basis, picked),
        (sel(2),),
        24,
        1_000_000_000,
    )
    x_got = lax.ppermute(x_send, "xl", SWAP)
    g_keep = call(
        grads_keep_kernel,
        "grads_keep",
        sds((4 * SLOT, WIDTH), F32),
        (slots, out_grads, grad_basis, near),
        (sel(4),),
        flops=600_000_000,
        behind=1,
    )
    z_keep, x_keep = call(
        acts_keep_kernel,
        "acts_keep",
        (blk(F32, 2, AZ), sds((4 * SLOT, AX), F32)),
        (picked, near, act_basis),
        flops=1_000_000_000,
    )

    x_own, *x_next = call(
        x_mid_kernel,
        "x_mid",
        (blk(F32, WIDTH + AX),) + (blk(I16, WIDTH + AX),) * 3,
        (g_keep, g_got, x_keep, x_got),
        (pltpu.VMEM((3, SLOT, WIDTH + AX), F32),),
    )
    x_last = [lax.ppermute(s, "z", ring(d)) for s, d in zip(x_next, HOPS)]
    z_own, z_next = call(z_mid_kernel, "z_mid", (blk(F32, AZ), blk(I16, AZ)), (z_keep, *z_got, x_own), behind=1)
    z_last = lax.ppermute(z_next, "xl", SWAP)

    def over(r):
        return lax.ppermute(r, "core", SWAP)

    rot_z = call(z_end_kernel, "z_end", blk(BF, AZ), (z_own, z_last), flops=2_000_000_000)
    z_mate = over(rot_z)
    z_far = lax.ppermute(rot_z, "y", ring(2))
    z_both = call(both_kernel, "z_both", blk(BF, 2, AZ), (rot_z, z_mate))
    z_side = lax.ppermute(z_both, ("y", "core"), SIDES)
    all_z = (rot_z, z_mate, z_far, over(z_far), z_side, over(z_side))
    rot_x = call(x_end_kernel, "x_end", blk(BF, WIDTH + AX), (x_own, *x_last, bad), flops=2_000_000_000)
    near = [rot_x] + [lax.ppermute(rot_x, "y", ring(d)) for d in (1, 3, 2)]
    all_x = [r for n in near for r in (n, over(n))]

    rows = pltpu.VMEM((GATHERED * PAD, WIDTH), BF)
    parts, whole = call(
        lambda *refs: gram_kernel(scale, *refs),
        "gram",
        (sds((16, 64, 384), BF), sds((8, 128), F32)),
        (*all_x, *all_z),
        (rows, rows),
        flops=600_000_000,
    )
    got = lax.all_to_all(parts, ("xh", "z", "xl"), 0, 0, tiled=True)
    return got, whole[0, 0] + lax.ppermute(whole, "xh", SWAP)[0, 0]


DP = ("y", "xh", "core")
TENSOR = ("z", "xl")


def general(hidden_acts, act_basis, out_grads, grad_basis, routed):
    tokens, width = hidden_acts.shape[0], act_basis.shape[1]
    own = tokens // 8

    def rotated(values, basis):
        part = jnp.dot(values, basis, preferred_element_type=F32).reshape(8, own, width)
        return jnp.sum(lax.all_to_all(part, TENSOR, 0, 0, tiled=True), axis=0).astype(BF)

    def shared(left, right):
        term = lax.dot_general(left, right, CONTRACT, preferred_element_type=F32) * (1.0 / (tokens * 16))
        blocks = term.reshape(16, width // 16, 8, width // 8).transpose(0, 2, 1, 3).reshape(128, width // 16, width // 8)
        return jnp.sum(lax.all_to_all(blocks, DP + TENSOR, 0, 0, tiled=True), axis=0)

    place = lax.axis_index("z") * 2 + lax.axis_index("xl")
    weights = lax.dynamic_slice_in_dim(routed, place * own, own, 0).astype(F32)[:, None]
    rot_acts, rot_grads = rotated(hidden_acts, act_basis), rotated(out_grads, grad_basis)
    acts_f, grads_f = rot_acts.astype(F32), rot_grads.astype(F32)
    return (
        shared((acts_f * weights).astype(BF), rot_acts),
        shared((grads_f * weights).astype(BF), rot_grads),
        shared((acts_f * acts_f * weights).astype(BF), (grads_f * grads_f).astype(BF)),
    )


def shards(*args):
    got, whole = fast(*args)

    def total(got, *_):
        return tuple(call(final_kernel, "final", (sds((64, 128), F32),) * 3, (got,)))

    return lax.cond(whole > 1.5, total, lambda _, *rest: general(*rest), got, *args)


def solution(mesh):
    fine = Mesh(mesh.devices.reshape(4, 2, 2, 4, 2), ("y", "xh", "core", "z", "xl"))
    return jax.shard_map(
        shards,
        mesh=fine,
        in_specs=(P(DP, TENSOR), P(TENSOR, None), P(DP, TENSOR), P(TENSOR, None), P(DP)),
        out_specs=(P(DP, TENSOR),) * 3,
        check_vma=False,
    )
```
